32 devices in a mesh: tok: 8 (over z, x), ch: 4 (over y, core).
Axes of the slice: x: 2, y: 2, z: 4, core: 2. Of those that a mesh axis runs over, the one named last changes fastest.
Arguments:
- tokens: bfloat16 [262144, 1024], P('tok', 'ch'), may hold values from -6 to 6
- w_value: bfloat16 [1024, 1024], P(None, 'ch'), may hold values from -0.1875 to 0.1875
- w_gate: bfloat16 [1024, 1024], P(None, 'ch'), may hold values from -0.1875 to 0.1875
- first_factor: bfloat16 [512, 512], replicated, may hold values from -0.25 to 0.25
- twiddle: float32 [512, 512], P('tok'), may hold values from 0.5 to 1.5
- second_factor: float32 [512, 512], replicated, may hold values from -0.25 to 0.25
- freq_kernel: float32 [512, 1024], P('tok', 'ch'), may hold values from -5 to 5
- row_kernel: float32 [512, 1024], P(None, 'ch'), may hold values from -5 to 5
- inverse_first: float32 [512, 512], replicated, may hold values from -0.25 to 0.25
- inverse_second: float32 [512, 512], replicated, may hold values from -0.25 to 0.25
Outputs:
- mixed: bfloat16 [262144, 1024], P('tok', 'ch')
The draws below stay inside these ranges and needn't reach their ends.
All inputs are finite; a program needn't handle non-finite values.
Results may differ from the reference program's by a relative error of at most 0.0049.
Values may be sent and summed in bfloat16 or wider, within the bound.
No kernel may reach another device: no remote copies, remote signals or barrier semaphores. Data moves between devices by JAX's collectives and lax.ppermute only.
A program may use at most 192 MiB of HBM per device.

```python
import math
import jax
import jax.numpy as jnp
from jax import lax

D = 1024
BLOCK_A = 512
BLOCK_B = 512
SEQ = 262144


def block_scale(rng, shape, cuts, low, top_value):
    def one(axis_at, shards_of):
        draws = jax.random.uniform(jax.random.fold_in(jax.random.fold_in(rng, 6), axis_at), (shards_of,), jnp.float32, low / len(cuts), top_value / len(cuts))
        return jnp.repeat(jnp.exp(draws), shape[axis_at] // shards_of).reshape((-1,) + (1,) * (len(shape) - axis_at - 1))

    level = one(*cuts[0])
    for cut in cuts[1:]:
        level = level * one(*cut)
    return level


def centred(own_key, dims, deviation, most, split=(), kind=jnp.bfloat16):
    values = deviation * jax.random.normal(own_key, dims, jnp.float32)
    if split:
        values = values * block_scale(own_key, dims, split, -0.22, 0.18)
    return jnp.clip(values, -most, most).astype(kind)


def setup_inputs(seed: int = 0) -> dict:
    key_list = jax.random.split(jax.random.key(seed), 11)
    return {
        "tokens": centred(key_list[0], (SEQ, D), 1.0, 6.0, ((0, 8), (1, 4))),
        "w_value": centred(key_list[1], (D, D), D ** -0.5, 0.1875, ((1, 4),)),
        "w_gate": centred(key_list[2], (D, D), D ** -0.5, 0.1875, ((1, 4),)),
        "first_factor": centred(key_list[3], (BLOCK_B, BLOCK_B), BLOCK_B ** -0.5, 0.25),
        "twiddle": jnp.clip(0.5 + 1.0 * jax.random.uniform(key_list[4], (BLOCK_A, BLOCK_B), jnp.float32) ** block_scale(key_list[4], (BLOCK_A, BLOCK_B), ((0, 8),), -0.2, 0.2), 0.5, 1.5),
        "second_factor": centred(key_list[5], (BLOCK_A, BLOCK_A), BLOCK_A ** -0.5, 0.25, (), jnp.float32),
        "freq_kernel": centred(key_list[6], (BLOCK_B, D), 1.0, 5.0, ((0, 8), (1, 4)), jnp.float32),
        "row_kernel": centred(key_list[7], (BLOCK_A, D), 1.0, 5.0, ((1, 4),), jnp.float32),
        "inverse_first": centred(key_list[8], (BLOCK_A, BLOCK_A), BLOCK_A ** -0.5, 0.25, (), jnp.float32),
        "inverse_second": centred(key_list[9], (BLOCK_B, BLOCK_B), BLOCK_B ** -0.5, 0.25, (), jnp.float32),
    }


def reference(tokens, w_value, w_gate, first_factor, twiddle, second_factor, freq_kernel, row_kernel, inverse_first, inverse_second):
    width = math.gcd(D, 128)
    count = D // width
    highest = lax.Precision.HIGHEST
    first_wide = first_factor.astype(jnp.float32)

    def split_cols(matrix):
        return matrix.reshape(matrix.shape[0], count, width).transpose(1, 0, 2)

    def one_block(pieces):
        value_cols, gate_cols, freq_cols, row_cols = pieces
        value = jnp.dot(tokens, value_cols, preferred_element_type=jnp.float32)
        gate = jnp.dot(tokens, gate_cols, preferred_element_type=jnp.float32)
        gated = (value * jax.nn.silu(gate)).astype(jnp.bfloat16).reshape(BLOCK_A, BLOCK_B, width)
        section = jnp.einsum('kb,abc->akc', first_wide, gated.astype(jnp.float32), precision=highest)
        section = section * twiddle[:, :, None]
        section = jnp.einsum('ja,akc->jkc', second_factor, section, precision=highest)
        section = section * freq_cols[None, :, :] * row_cols[:, None, :]
        section = jnp.einsum('ij,jkc->ikc', inverse_first, section, precision=highest)
        result = jnp.einsum('bk,akc->abc', inverse_second, section, precision=highest)
        return result.reshape(SEQ, width).astype(jnp.bfloat16)

    blocks = lax.map(one_block, (split_cols(w_value), split_cols(w_gate), split_cols(freq_kernel), split_cols(row_kernel)))
    return blocks.transpose(1, 0, 2).reshape(SEQ, D)
```

```python
import functools

import jax
import jax.numpy as jnp
from jax import lax
from jax.experimental import pallas as pl
from jax.experimental.pallas import tpu as pltpu
from jax.sharding import PartitionSpec as P

BLOCK = 512
GROUP = 16
HALF = 128
STEP = 2
VMEM = 56 * 2**20


def params():
    return pltpu.CompilerParams(vmem_limit_bytes=VMEM, dimension_semantics=("arbitrary",))


def wide_dot(left, right):
    return jnp.dot(left, right, preferred_element_type=jnp.float32)


def two_parts(matrix):
    upper = lax.reduce_precision(matrix, 8, 7)
    return jnp.concatenate([upper.astype(jnp.bfloat16), (matrix - upper).astype(jnp.bfloat16)], axis=0)


def split_dot(stacked, right):
    both = wide_dot(stacked, right)
    rows = both.shape[0] // 2
    return both[:rows] + both[rows:]


def first_body(halves, x_ref, w_ref, factor_ref, twiddle_ref, *rest):
    outs, scratch = rest[:-2], rest[-2:]
    step = pl.program_id(0)
    channels = w_ref.shape[1] // 2
    both = wide_dot(x_ref[...], w_ref[...])
    value, gate = both[:, :channels], both[:, channels:]
    gated = (value * (gate / (1.0 + jnp.exp(-gate)))).astype(jnp.bfloat16)
    for row in range(STEP):
        section = wide_dot(factor_ref[...], gated[row * BLOCK : (row + 1) * BLOCK])
        section = section * twiddle_ref[0, :, row : row + 1]
        for half in range(2):
            scratch[half][pl.ds(step * STEP + row, BLOCK, stride=GROUP), :] = section[:, half * HALF : (half + 1) * HALF]

    @pl.when(step == pl.num_programs(0) - 1)
    def _():
        parts, inner = outs[0].shape[0], outs[0].shape[1]
        size = inner * GROUP

        @pl.loop(0, parts)
        def _(part):
            for half in range(2):
                tile = scratch[half][pl.ds(part * size, size), :].astype(jnp.bfloat16).reshape(inner, GROUP, HALF)
                if halves:
                    outs[half][part] = tile
                else:
                    outs[0][part, :, :, half * HALF : (half + 1) * HALF] = tile


def first_section(x, w, factor, twiddle, parts, halves):
    rows = x.shape[0] // BLOCK
    steps = rows // STEP
    inner = BLOCK // parts
    channels = w.shape[1] // 2
    columns = twiddle.reshape(steps, STEP, BLOCK).transpose(0, 2, 1)
    widths = [HALF, HALF] if halves else [channels]
    outs = [jax.ShapeDtypeStruct((parts, inner, rows, width), jnp.bfloat16) for width in widths]
    return pl.pallas_call(
        functools.partial(first_body, halves),
        grid=(steps,),
        in_specs=[
            pl.BlockSpec((STEP * BLOCK, x.shape[1]), lambda s: (s, 0)),
            pl.BlockSpec(w.shape, lambda s: (0, 0)),
            pl.BlockSpec(factor.shape, lambda s: (0, 0)),
            pl.BlockSpec((1, BLOCK, STEP), lambda s: (s, 0, 0)),
        ],
        out_specs=[pl.BlockSpec(out.shape, lambda s: (0, 0, 0, 0)) for out in outs],
        out_shape=outs,
        scratch_shapes=[pltpu.VMEM((BLOCK * rows, HALF), jnp.float32)] * 2,
        compiler_params=params(),
        cost_estimate=pl.CostEstimate(
            flops=2 * x.shape[0] * channels * (2 * x.shape[1] + BLOCK),
            bytes_accessed=2 * x.size + 2 * x.shape[0] * channels,
            transcendentals=x.shape[0] * channels,
        ),
        name="project_and_mix_rows",
    )(x, w, factor, columns)


def middle_body(count, *refs):
    blocks = refs[:count]
    second_ref, inverse_ref, freq_ref, row_ref, out_ref, scratch = refs[count:]

    @pl.loop(0, GROUP // 2)
    def _(pair):
        sides = []
        for side in range(2):
            tiles = [block[:, 2 * pair + side].reshape(-1, HALF) for block in blocks]
            sides.append(jnp.concatenate(tiles, axis=0))
        section = split_dot(second_ref[...], jnp.concatenate(sides, axis=1))
        spectrum = jnp.concatenate(
            [
                section[:, side * HALF : (side + 1) * HALF] * freq_ref[pl.ds(2 * pair + side, 1), :] * row_ref[...]
                for side in range(2)
            ],
            axis=1,
        )
        section = split_dot(inverse_ref[...], spectrum.astype(jnp.bfloat16))
        for side in range(2):
            scratch[pl.ds(2 * pair + side, BLOCK, stride=GROUP), :] = section[:, side * HALF : (side + 1) * HALF]

    parts, inner = out_ref.shape[0], out_ref.shape[1]
    size = inner * GROUP

    @pl.loop(0, parts)
    def _(part):
        out_ref[part] = scratch[pl.ds(part * size, size), :].astype(jnp.bfloat16).reshape(inner, GROUP, HALF)


def middle_section(blocks, at, second, inverse, freq, row, parts):
    indices = freq.shape[0]
    inner = BLOCK // parts
    specs = [pl.BlockSpec((parts, GROUP, GROUP, HALF), lambda s, at=where: (0, s, 0, at)) for where in at]
    out = jax.ShapeDtypeStruct((parts, inner, indices, HALF), jnp.bfloat16)
    return pl.pallas_call(
        functools.partial(middle_body, len(blocks)),
        grid=(indices // GROUP,),
        in_specs=specs
        + [
            pl.BlockSpec(second.shape, lambda s: (0, 0)),
            pl.BlockSpec(inverse.shape, lambda s: (0, 0)),
            pl.BlockSpec((GROUP, HALF), lambda s: (s, 0)),
            pl.BlockSpec(row.shape, lambda s: (0, 0)),
        ],
        out_specs=pl.BlockSpec((parts, inner, GROUP, HALF), lambda s: (0, 0, s, 0)),
        out_shape=out,
        scratch_shapes=[pltpu.VMEM((BLOCK * GROUP, HALF), jnp.float32)],
        compiler_params=params(),
        cost_estimate=pl.CostEstimate(
            flops=8 * BLOCK * BLOCK * indices * HALF,
            bytes_accessed=4 * BLOCK * indices * HALF,
            transcendentals=0,
        ),
        name="mix_grid_rows",
    )(*blocks, second, inverse, freq, row)


def last_body(x_ref, inverse_ref, *rest):
    out_ref = rest[-1]

    @pl.loop(0, x_ref.shape[1] // 2)
    def _(pair):
        sides = [x_ref[:, 2 * pair + side].reshape(BLOCK, HALF) for side in range(2)]
        mixed = split_dot(inverse_ref[...], jnp.concatenate(sides, axis=1)).astype(jnp.bfloat16)
        for side in range(2):
            start = pl.multiple_of((2 * pair + side) * BLOCK, BLOCK)
            out_ref[pl.ds(start, BLOCK), :] = mixed[:, side * HALF : (side + 1) * HALF]


def last_section(x, inverse, shape, half, before):
    parts, rows, inner, _ = x.shape
    group = 8
    operands = [x, inverse]
    specs = [
        pl.BlockSpec((parts, group, inner, HALF), lambda s: (0, s, 0, 0)),
        pl.BlockSpec(inverse.shape, lambda s: (0, 0)),
    ]
    aliases = {}
    if before is not None:
        operands.append(before)
        specs.append(pl.BlockSpec(memory_space=pl.ANY))
        aliases = {2: 0}
    return pl.pallas_call(
        last_body,
        grid=(rows // group,),
        in_specs=specs,
        out_specs=pl.BlockSpec((group * BLOCK, HALF), lambda s: (s, half)),
        out_shape=jax.ShapeDtypeStruct(shape, jnp.bfloat16),
        input_output_aliases=aliases,
        compiler_params=params(),
        cost_estimate=pl.CostEstimate(
            flops=4 * BLOCK * BLOCK * rows * HALF,
            bytes_accessed=4 * BLOCK * rows * HALF,
            transcendentals=0,
        ),
        name="mix_rows_back",
    )(*operands)


def shards(
    parts,
    tokens,
    w_value,
    w_gate,
    first_factor,
    twiddle,
    second_factor,
    freq_kernel,
    row_kernel,
    inverse_first,
    inverse_second,
):
    tok_rows, channels = tokens.shape
    local_rows = tok_rows // BLOCK
    chunks = local_rows // GROUP
    weights = jnp.concatenate([w_value, w_gate], axis=1)
    second = second_factor.reshape(BLOCK, parts, chunks, GROUP).transpose(0, 2, 1, 3).reshape(BLOCK, BLOCK)
    second, inverse, back = two_parts(second), two_parts(inverse_first), two_parts(inverse_second)

    def exchange(x):
        return lax.all_to_all(x, "tok", split_axis=0, concat_axis=0, tiled=True)

    blocks = [[], []]
    places = [[], []]
    own = before = None
    for chunk in range(chunks):
        rows = slice(chunk * GROUP * BLOCK, (chunk + 1) * GROUP * BLOCK)
        source = tokens if own is None else lax.optimization_barrier((tokens, own))[0]
        own = source[rows]
        piece = lax.all_gather(own, "ch", axis=1, tiled=True)
        last = chunk == chunks - 1
        outs = first_section(
            piece, weights, first_factor, twiddle[chunk * GROUP : (chunk + 1) * GROUP], parts, last
        )
        moved = []
        for out in outs:
            before = out if before is None else lax.optimization_barrier((out, before))[0]
            before = exchange(before)
            moved.append(before)
        for half in range(2):
            blocks[half].append(moved[half] if last else moved[0])
            places[half].append(0 if last else half)

    moved = []
    for half in range(2):
        lanes = slice(half * HALF, (half + 1) * HALF)
        section = middle_section(
            blocks[half], places[half], second, inverse, freq_kernel[:, lanes], row_kernel[:, lanes], parts
        )
        moved.append(exchange(section))
    result = None
    for half in range(2):
        result = last_section(moved[half], back, (tok_rows, channels), half, result)
    return result


def solution(mesh):
    return jax.shard_map(
        functools.partial(shards, mesh.shape["tok"]),
        mesh=mesh,
        in_specs=(
            P("tok", "ch"),
            P(None, "ch"),
            P(None, "ch"),
            P(),
            P("tok", None),
            P(),
            P("tok", "ch"),
            P(None, "ch"),
            P(),
            P(),
        ),
        out_specs=P("tok", "ch"),
        check_vma=False,
    )
```

```python
import functools

import jax
import jax.numpy as jnp
from jax import lax
from jax.experimental import pallas as pl
from jax.experimental.pallas import tpu as pltpu
from jax.sharding import PartitionSpec as P

BLOCK = 512
GROUP = 16
HALF = 128
STEP = 2
VMEM = 56 * 2**20


def params():
    return pltpu.CompilerParams(vmem_limit_bytes=VMEM, dimension_semantics=("arbitrary",))


def wide_dot(left, right):
    return jnp.dot(left, right, preferred_element_type=jnp.float32)


def two_parts(matrix):
    upper = lax.reduce_precision(matrix, 8, 7)
    return jnp.concatenate([upper.astype(jnp.bfloat16), (matrix - upper).astype(jnp.bfloat16)], axis=0)


def split_dot(stacked, right):
    both = wide_dot(stacked, right)
    rows = both.shape[0] // 2
    return both[:rows] + both[rows:]


def first_body(count, halves, *refs):
    pieces, (w_ref, factor_ref, twiddle_ref, *rest) = refs[:count], refs[count:]
    outs, scratch = rest[:-2], rest[-2:]
    step = pl.program_id(0)
    channels = w_ref.shape[1] // 2
    both = wide_dot(jnp.concatenate([piece[...] for piece in pieces], axis=1), w_ref[...])
    value, gate = both[:, :channels], both[:, channels:]
    gated = (value * (gate / (1.0 + jnp.exp(-gate)))).astype(jnp.bfloat16)
    for row in range(STEP):
        section = wide_dot(factor_ref[...], gated[row * BLOCK : (row + 1) * BLOCK])
        section = section * twiddle_ref[0, :, row : row + 1]
        for half in range(2):
            scratch[half][pl.ds(step * STEP + row, BLOCK, stride=GROUP), :] = section[:, half * HALF : (half + 1) * HALF]

    @pl.when(step == pl.num_programs(0) - 1)
    def _():
        parts, inner = outs[0].shape[0], outs[0].shape[1]
        size = inner * GROUP

        @pl.loop(0, parts)
        def _(part):
            for half in range(2):
                tile = scratch[half][pl.ds(part * size, size), :].astype(jnp.bfloat16).reshape(inner, GROUP, HALF)
                if halves:
                    outs[half][part] = tile
                else:
                    outs[0][part, :, :, half * HALF : (half + 1) * HALF] = tile


def first_section(pieces, begin, w, factor, twiddle, parts, halves):
    rows = twiddle.shape[0]
    depth, patches = w.shape[0], rows * BLOCK
    steps = rows // STEP
    inner = BLOCK // parts
    channels = w.shape[1] // 2
    columns = twiddle.reshape(steps, STEP, BLOCK).transpose(0, 2, 1)
    widths = [HALF, HALF] if halves else [channels]
    outs = [jax.ShapeDtypeStruct((parts, inner, rows, width), jnp.bfloat16) for width in widths]
    return pl.pallas_call(
        functools.partial(first_body, len(pieces), halves),
        grid=(steps,),
        in_specs=[
            pl.BlockSpec((STEP * BLOCK, piece.shape[1]), lambda s, at=at: (at // STEP + s, 0))
            for piece, at in zip(pieces, [begin] + [0] * len(pieces))
        ]
        + [
            pl.BlockSpec(w.shape, lambda s: (0, 0)),
            pl.BlockSpec(factor.shape, lambda s: (0, 0)),
            pl.BlockSpec((1, BLOCK, STEP), lambda s: (s, 0, 0)),
        ],
        out_specs=[pl.BlockSpec(out.shape, lambda s: (0, 0, 0, 0)) for out in outs],
        out_shape=outs,
        scratch_shapes=[pltpu.VMEM((BLOCK * rows, HALF), jnp.float32)] * 2,
        compiler_params=params(),
        cost_estimate=pl.CostEstimate(
            flops=2 * patches * channels * (2 * depth + BLOCK),
            bytes_accessed=2 * patches * (depth + channels),
            transcendentals=patches * channels,
        ),
        name="project_and_mix_rows",
    )(*pieces, w, factor, columns)


def middle_body(count, *refs):
    blocks = refs[:count]
    second_ref, inverse_ref, freq_ref, row_ref, out_ref, scratch = refs[count:]

    @pl.loop(0, GROUP // 2)
    def _(pair):
        sides = []
        for side in range(2):
            tiles = [block[:, 2 * pair + side].reshape(-1, HALF) for block in blocks]
            sides.append(jnp.concatenate(tiles, axis=0))
        section = split_dot(second_ref[...], jnp.concatenate(sides, axis=1))
        spectrum = jnp.concatenate(
            [
                section[:, side * HALF : (side + 1) * HALF] * freq_ref[pl.ds(2 * pair + side, 1), :] * row_ref[...]
                for side in range(2)
            ],
            axis=1,
        )
        section = split_dot(inverse_ref[...], spectrum.astype(jnp.bfloat16))
        for side in range(2):
            scratch[pl.ds(2 * pair + side, BLOCK, stride=GROUP), :] = section[:, side * HALF : (side + 1) * HALF]

    parts, inner = out_ref.shape[0], out_ref.shape[1]
    size = inner * GROUP

    @pl.loop(0, parts)
    def _(part):
        out_ref[part] = scratch[pl.ds(part * size, size), :].astype(jnp.bfloat16).reshape(inner, GROUP, HALF)


def middle_section(blocks, at, second, inverse, freq, row, parts):
    indices = freq.shape[0]
    inner = BLOCK // parts
    specs = [pl.BlockSpec((parts, GROUP, GROUP, HALF), lambda s, at=where: (0, s, 0, at)) for where in at]
    out = jax.ShapeDtypeStruct((parts, inner, indices, HALF), jnp.bfloat16)
    return pl.pallas_call(
        functools.partial(middle_body, len(blocks)),
        grid=(indices // GROUP,),
        in_specs=specs
        + [
            pl.BlockSpec(second.shape, lambda s: (0, 0)),
            pl.BlockSpec(inverse.shape, lambda s: (0, 0)),
            pl.BlockSpec((GROUP, HALF), lambda s: (s, 0)),
            pl.BlockSpec(row.shape, lambda s: (0, 0)),
        ],
        out_specs=pl.BlockSpec((parts, inner, GROUP, HALF), lambda s: (0, 0, s, 0)),
        out_shape=out,
        scratch_shapes=[pltpu.VMEM((BLOCK * GROUP, HALF), jnp.float32)],
        compiler_params=params(),
        cost_estimate=pl.CostEstimate(
            flops=8 * BLOCK * BLOCK * indices * HALF,
            bytes_accessed=4 * BLOCK * indices * HALF,
            transcendentals=0,
        ),
        name="mix_grid_rows",
    )(*blocks, second, inverse, freq, row)


def last_body(x_ref, inverse_ref, *rest):
    out_ref = rest[-1]

    @pl.loop(0, x_ref.shape[1] // 2)
    def _(pair):
        sides = [x_ref[:, 2 * pair + side].reshape(BLOCK, HALF) for side in range(2)]
        mixed = split_dot(inverse_ref[...], jnp.concatenate(sides, axis=1)).astype(jnp.bfloat16)
        for side in range(2):
            start = pl.multiple_of((2 * pair + side) * BLOCK, BLOCK)
            out_ref[pl.ds(start, BLOCK), :] = mixed[:, side * HALF : (side + 1) * HALF]


def last_section(x, inverse, shape, half, before):
    parts, rows, inner, _ = x.shape
    group = 8
    operands = [x, inverse]
    specs = [
        pl.BlockSpec((parts, group, inner, HALF), lambda s: (0, s, 0, 0)),
        pl.BlockSpec(inverse.shape, lambda s: (0, 0)),
    ]
    aliases = {}
    if before is not None:
        operands.append(before)
        specs.append(pl.BlockSpec(memory_space=pl.ANY))
        aliases = {2: 0}
    return pl.pallas_call(
        last_body,
        grid=(rows // group,),
        in_specs=specs,
        out_specs=pl.BlockSpec((group * BLOCK, HALF), lambda s: (s, half)),
        out_shape=jax.ShapeDtypeStruct(shape, jnp.bfloat16),
        input_output_aliases=aliases,
        compiler_params=params(),
        cost_estimate=pl.CostEstimate(
            flops=4 * BLOCK * BLOCK * rows * HALF,
            bytes_accessed=4 * BLOCK * rows * HALF,
            transcendentals=0,
        ),
        name="mix_rows_back",
    )(*operands)


def swap(x, count, bit):
    return lax.ppermute(x, "ch", [(at, at ^ bit) for at in range(count)])


def shards(
    parts,
    sides,
    tokens,
    w_value,
    w_gate,
    first_factor,
    twiddle,
    second_factor,
    freq_kernel,
    row_kernel,
    inverse_first,
    inverse_second,
):
    tok_rows, channels = tokens.shape
    local_rows = tok_rows // BLOCK
    chunks = local_rows // GROUP
    order = [0]
    bits = [sides >> step for step in range(1, sides.bit_length())]
    for bit in bits:
        order = order + [at ^ bit for at in order]
    weights = jnp.concatenate([w_value, w_gate], axis=1).reshape(sides, channels, -1)
    weights = weights[lax.axis_index("ch") ^ jnp.array(order)].reshape(sides * channels, -1)
    second = second_factor.reshape(BLOCK, parts, chunks, GROUP).transpose(0, 2, 1, 3).reshape(BLOCK, BLOCK)
    second, inverse, back = two_parts(second), two_parts(inverse_first), two_parts(inverse_second)

    def exchange(x):
        return lax.all_to_all(x, "tok", split_axis=0, concat_axis=0, tiled=True)

    blocks = [[], []]
    places = [[], []]
    own = before = None
    for chunk in range(chunks):
        rows = slice(chunk * GROUP * BLOCK, (chunk + 1) * GROUP * BLOCK)
        source = tokens if own is None else lax.optimization_barrier((tokens, own))[0]
        own = source[rows]
        pieces = [own]
        for bit in bits:
            pieces = pieces + [swap(piece, sides, bit) for piece in pieces]
        pieces[0] = tokens
        last = chunk == chunks - 1
        outs = first_section(
            pieces, chunk * GROUP, weights, first_factor, twiddle[chunk * GROUP : (chunk + 1) * GROUP], parts, last
        )
        moved = []
        for out in outs:
            before = out if before is None else lax.optimization_barrier((out, before))[0]
            before = exchange(before)
            moved.append(before)
        for half in range(2):
            blocks[half].append(moved[half] if last else moved[0])
            places[half].append(0 if last else half)

    moved = []
    for half in range(2):
        lanes = slice(half * HALF, (half + 1) * HALF)
        section = middle_section(
            blocks[half], places[half], second, inverse, freq_kernel[:, lanes], row_kernel[:, lanes], parts
        )
        moved.append(exchange(section))
    result = None
    for half in range(2):
        result = last_section(moved[half], back, (tok_rows, channels), half, result)
    return result


def solution(mesh):
    return jax.shard_map(
        functools.partial(shards, mesh.shape["tok"], mesh.shape["ch"]),
        mesh=mesh,
        in_specs=(
            P("tok", "ch"),
            P(None, "ch"),
            P(None, "ch"),
            P(),
            P("tok", None),
            P(),
            P("tok", "ch"),
            P(None, "ch"),
            P(),
            P(),
        ),
        out_specs=P("tok", "ch"),
        check_vma=False,
    )
```

```python
import functools

import jax
import jax.numpy as jnp
from jax import lax
from jax.experimental import pallas as pl
from jax.experimental.pallas import tpu as pltpu
from jax.sharding import PartitionSpec as P

BLOCK = 512
CHUNK = 8
GROUP = 16
HALF = 128
STEP = 2
WIDE = 4
VMEM = 56 * 2**20

WHOLE = pl.BlockSpec(memory_space=pltpu.SMEM)


def params():
    return pltpu.CompilerParams(vmem_limit_bytes=VMEM, dimension_semantics=("arbitrary",))


def full(array):
    return pl.BlockSpec(array.shape, lambda s: (0,) * array.ndim)


def wide_dot(left, right):
    return jnp.dot(left, right, preferred_element_type=jnp.float32)


def store_parts(parts_ref, matrix_ref):
    rows = matrix_ref.shape[0]
    matrix = matrix_ref[...]
    upper = matrix.astype(jnp.bfloat16)
    parts_ref[:rows] = upper
    parts_ref[rows:] = (matrix - upper.astype(jnp.float32)).astype(jnp.bfloat16)


def split_dot(parts_ref, right):
    both = wide_dot(parts_ref[...], right)
    rows = both.shape[0] // 2
    return both[:rows] + both[rows:]


def put(outs, half, halves, partner, parts, block):
    lanes = slice(None) if halves else slice(half * HALF, (half + 1) * HALF)
    one_array = len(outs) == (2 if halves else 1)
    if one_array:
        outs[half if halves else 0][partner, :, lanes] = block
    else:
        outs[half * parts + partner if halves else partner][:, lanes] = block


def place_of(device, partner, together):
    return partner if together else device ^ partner


def first_body(order, parts, halves, together, at_ref, *refs):
    count = len(refs) - 8 - (1 if together else parts) * (2 if halves else 1)
    pieces, (value_ref, gate_ref, factor_ref, twiddle_ref) = refs[:count], refs[count : count + 4]
    outs, (scratch_a, scratch_b, weights, columns) = refs[count + 4 : -4], refs[-4:]
    scratch = (scratch_a, scratch_b)
    step = pl.program_id(0)
    channels = value_ref.shape[1]
    rows = twiddle_ref.shape[0]

    @pl.when(step == 0)
    def _():
        for place, (keep, flip) in enumerate(order):
            begin = pl.multiple_of(((at_ref[1] & keep) ^ flip) * channels, channels)
            here = slice(place * channels, (place + 1) * channels)
            weights[here, :channels] = value_ref[pl.ds(begin, channels), :]
            weights[here, channels:] = gate_ref[pl.ds(begin, channels), :]
        padding = jnp.zeros((128 - rows, BLOCK), jnp.float32)
        columns[...] = jnp.concatenate([twiddle_ref[...], padding], axis=0).T

    both = wide_dot(jnp.concatenate([piece[...] for piece in pieces], axis=1), weights[...])
    value, gate = both[:, :channels], both[:, channels:]
    gated = (value * (gate / (1.0 + jnp.exp(-gate)))).astype(jnp.bfloat16)
    lanes = lax.broadcasted_iota(jnp.int32, columns.shape, 1)
    for row in range(STEP):
        at = step * STEP + row
        scale = jnp.sum(jnp.where(lanes == at, columns[...], 0.0), axis=1, keepdims=True)
        section = wide_dot(factor_ref[...], gated[row * BLOCK : (row + 1) * BLOCK]) * scale
        for half in range(2):
            scratch[half][pl.ds(at, BLOCK, stride=rows), :] = section[:, half * HALF : (half + 1) * HALF]

    @pl.when(step == pl.num_programs(0) - 1)
    def _():
        size = BLOCK // parts * rows
        for partner in range(parts):
            begin = pl.multiple_of(place_of(at_ref[0], partner, together) * size, size)
            for half in range(2):
                put(outs, half, halves, partner, parts, scratch[half][pl.ds(begin, size), :].astype(jnp.bfloat16))


def first_section(at, pieces, order, begin, rows, w_value, w_gate, factor, twiddle, parts, halves, together):
    channels = w_value.shape[1]
    depth, patches = w_value.shape[0], rows * BLOCK
    inner = BLOCK // parts
    widths = [HALF] * 2 if halves else [channels]
    if together:
        outs = [jax.ShapeDtypeStruct((parts, inner * rows, width), jnp.bfloat16) for width in widths]
    else:
        outs = [jax.ShapeDtypeStruct((inner * rows, width), jnp.bfloat16) for width in widths for _ in range(parts)]
    return pl.pallas_call(
        functools.partial(first_body, order, parts, halves, together),
        grid=(rows // STEP,),
        in_specs=[WHOLE]
        + [
            pl.BlockSpec((STEP * BLOCK, piece.shape[1]), lambda s: (s, 0)) for piece in pieces
        ]
        + [full(w_value), full(w_gate), full(factor), pl.BlockSpec((rows, BLOCK), lambda s: (begin // rows, 0))],
        out_specs=[full(out) for out in outs],
        out_shape=outs,
        scratch_shapes=[pltpu.VMEM((BLOCK * rows, HALF), jnp.float32)] * 2
        + [pltpu.VMEM((depth, 2 * channels), jnp.bfloat16), pltpu.VMEM((BLOCK, 128), jnp.float32)],
        compiler_params=params(),
        cost_estimate=pl.CostEstimate(
            flops=2 * patches * channels * (2 * depth + BLOCK),
            bytes_accessed=2 * patches * (depth + channels),
            transcendentals=patches * channels,
        ),
        name="project_and_mix_rows",
    )(at, *pieces, w_value, w_gate, factor, twiddle)


def middle_body(ways, parts, splits, together, at_ref, *refs):
    chunks = len(ways)
    blocks, count = [], 0
    for way in ways:
        blocks.append(refs[count : count + (1 if way else parts)])
        count += len(blocks[-1])
    second_ref, inverse_ref, freq_ref, row_ref = refs[count : count + 4]
    outs, (second, inverse, gathered, scratch) = refs[count + 4 : -4], refs[-4:]
    local_rows = chunks * CHUNK

    def tile_of(chunk, source, start):
        if ways[chunk]:
            return blocks[chunk][0][source, pl.ds(start, 2 * CHUNK), :].astype(jnp.float32)
        return blocks[chunk][source][pl.ds(start, 2 * CHUNK), :].astype(jnp.float32)

    @pl.when(pl.program_id(0) == 0)
    def _():
        store_parts(second, second_ref)
        store_parts(inverse, inverse_ref)

    @pl.loop(0, GROUP // 2)
    def _(pair):
        start = pl.multiple_of(pair * 2 * CHUNK, 2 * CHUNK)
        lane = pl.multiple_of(pair * 2 * HALF, 2 * HALF)
        for partner in range(parts):
            for chunk in range(0, chunks, 2):
                one, two = (tile_of(chunk + more, partner, start) for more in range(2))
                place = place_of(at_ref[0], partner, ways[chunk])
                row = pl.multiple_of(place * local_rows + chunk * CHUNK, 2 * CHUNK)
                for side in range(2):
                    here = slice(side * CHUNK, (side + 1) * CHUNK)
                    tile = jnp.concatenate([one[here], two[here]], axis=0).astype(jnp.bfloat16)
                    gathered[pl.ds(row, 2 * CHUNK), pl.ds(pl.multiple_of(lane + side * HALF, HALF), HALF)] = tile

    row_gate = jnp.concatenate([row_ref[...]] * WIDE, axis=1)

    @pl.loop(0, GROUP // WIDE)
    def _(turn):
        lane = pl.multiple_of(turn * WIDE * HALF, WIDE * HALF)
        section = split_dot(second, gathered[:, pl.ds(lane, WIDE * HALF)])
        freq = jnp.concatenate([freq_ref[pl.ds(turn * WIDE + side, 1), :] for side in range(WIDE)], axis=1)
        spectrum = (section * freq * row_gate).astype(jnp.bfloat16)
        section = split_dot(inverse, spectrum)
        for side in range(WIDE):
            scratch[pl.ds(turn * WIDE + side, BLOCK, stride=GROUP), :] = section[:, side * HALF : (side + 1) * HALF]

    size = BLOCK // parts // splits * GROUP
    for split in range(splits):
        for partner in range(parts):
            place = place_of(at_ref[0], partner, together)
            begin = pl.multiple_of(place * (size * splits) + split * size, size)
            block = scratch[pl.ds(begin, size), :].astype(jnp.bfloat16).reshape(size // GROUP, GROUP, HALF)
            if together:
                outs[split][partner] = block
            else:
                outs[split * parts + partner][...] = block


def middle_section(at, blocks, places, half, begin, indices, second, inverse, freq, row, parts, splits, together):
    inner = BLOCK // parts
    first = begin // GROUP
    ways = [len(chunk) == 1 for chunk in blocks]
    operands, specs = [], []
    for chunk, place in zip(blocks, places):
        for block in chunk:
            operands.append(block)
            if len(chunk) == 1:
                specs.append(pl.BlockSpec((parts, GROUP * CHUNK, HALF), lambda s, place=place: (0, first + s, place)))
            else:
                specs.append(pl.BlockSpec((GROUP * CHUNK, HALF), lambda s, place=place: (first + s, place)))
    if together:
        outs = [jax.ShapeDtypeStruct((parts, inner // splits, indices, HALF), jnp.bfloat16)] * splits
        out_specs = [pl.BlockSpec((parts, inner // splits, GROUP, HALF), lambda s: (0, 0, s, 0))] * len(outs)
    else:
        outs = [jax.ShapeDtypeStruct((inner // splits, indices, HALF), jnp.bfloat16)] * (parts * splits)
        out_specs = [pl.BlockSpec((inner // splits, GROUP, HALF), lambda s: (0, s, 0))] * len(outs)
    return pl.pallas_call(
        functools.partial(middle_body, ways, parts, splits, together),
        grid=(indices // GROUP,),
        in_specs=[WHOLE]
        + specs
        + [
            full(second),
            full(inverse),
            pl.BlockSpec((GROUP, HALF), lambda s: (first + s, half)),
            pl.BlockSpec((BLOCK, HALF), lambda s: (0, half)),
        ],
        out_specs=out_specs,
        out_shape=outs,
        scratch_shapes=[pltpu.VMEM((2 * BLOCK, BLOCK), jnp.bfloat16)] * 2
        + [pltpu.VMEM((BLOCK, GROUP * HALF), jnp.bfloat16), pltpu.VMEM((BLOCK * GROUP, HALF), jnp.float32)],
        compiler_params=params(),
        cost_estimate=pl.CostEstimate(
            flops=8 * BLOCK * BLOCK * indices * HALF,
            bytes_accessed=4 * BLOCK * indices * HALF,
            transcendentals=0,
        ),
        name="mix_grid_rows",
    )(at, *operands, second, inverse, freq, row)


def last_body(ways, starts, parts, at_ref, *refs):
    blocks, count = [], 0
    for way in ways:
        blocks.append(refs[count : count + (1 if way else parts)])
        count += len(blocks[-1])
    inverse_ref = refs[count]
    out_ref, inverse, gathered = refs[-3:]
    inner = BLOCK // parts
    group = blocks[0][0].shape[-3]

    @pl.when(pl.program_id(0) == 0)
    def _():
        store_parts(inverse, inverse_ref)

    for row in range(group):
        for partner in range(parts):
            for piece, start in enumerate(starts):
                block = blocks[piece][0].at[partner] if ways[piece] else blocks[piece][partner]
                begin = pl.multiple_of(place_of(at_ref[0], partner, ways[piece]) * inner + start, GROUP)
                gathered[pl.ds(begin, block.shape[1]), row * HALF : (row + 1) * HALF] = block[row]

    @pl.loop(0, group // WIDE)
    def _(turn):
        lane = pl.multiple_of(turn * WIDE * HALF, WIDE * HALF)
        mixed = split_dot(inverse, gathered[:, pl.ds(lane, WIDE * HALF)]).astype(jnp.bfloat16)
        for side in range(WIDE):
            start = pl.multiple_of((turn * WIDE + side) * BLOCK, BLOCK)
            out_ref[pl.ds(start, BLOCK), :] = mixed[:, side * HALF : (side + 1) * HALF]


def last_section(at, blocks, starts, parts, inverse, shape, begin, half, before):
    ways = [len(piece) == 1 for piece in blocks]
    rows = blocks[0][0].shape[-3]
    group = min(rows, 8)
    operands, specs = [at], [WHOLE]
    for block in [block for piece in blocks for block in piece]:
        operands.append(block)
        if block.ndim == 4:
            specs.append(pl.BlockSpec((parts, group, *block.shape[2:]), lambda s: (0, s, 0, 0)))
        else:
            specs.append(pl.BlockSpec((group, *block.shape[1:]), lambda s: (s, 0, 0)))
    operands.append(inverse)
    specs.append(full(inverse))
    aliases = {}
    if before is not None:
        aliases = {len(operands): 0}
        operands.append(before)
        specs.append(pl.BlockSpec(memory_space=pl.ANY))
    return pl.pallas_call(
        functools.partial(last_body, ways, starts, parts),
        grid=(rows // group,),
        in_specs=specs,
        out_specs=pl.BlockSpec((group * BLOCK, HALF), lambda s: (begin // group + s, half)),
        out_shape=jax.ShapeDtypeStruct(shape, jnp.bfloat16),
        input_output_aliases=aliases,
        scratch_shapes=[pltpu.VMEM((2 * BLOCK, BLOCK), jnp.bfloat16), pltpu.VMEM((BLOCK, group * HALF), jnp.bfloat16)],
        compiler_params=params(),
        cost_estimate=pl.CostEstimate(
            flops=4 * BLOCK * BLOCK * rows * HALF,
            bytes_accessed=4 * BLOCK * rows * HALF,
            transcendentals=0,
        ),
        name="mix_rows_back",
    )(*operands)


def swap(x, axis, count, bits):
    return lax.ppermute(x, axis, [(at, at ^ bits) for at in range(count)])


def exchange(blocks, parts):
    if len(blocks) == 1:
        return [lax.all_to_all(blocks[0], "tok", split_axis=0, concat_axis=0, tiled=True)]
    moved = list(blocks)
    for partner in range(parts - 1, 0, -1):
        moved[partner] = swap(blocks[partner], "tok", parts, partner)
    return moved


def after(x, before):
    return x if before is None else lax.optimization_barrier((x, before))[0]


def shards(
    parts,
    sides,
    tokens,
    w_value,
    w_gate,
    first_factor,
    twiddle,
    second_factor,
    freq_kernel,
    row_kernel,
    inverse_first,
    inverse_second,
):
    tok_rows, channels = tokens.shape
    local_rows = tok_rows // BLOCK
    chunks = local_rows // CHUNK
    inner = BLOCK // parts
    at = jnp.stack([lax.axis_index("tok"), lax.axis_index("ch")]).astype(jnp.int32)
    far = sides // 2
    pairs = [[side, side + far] for side in range(far)]
    bits = [far >> step for step in range(1, far.bit_length())]
    order = [(far - 1, 0), (far - 1, far)]
    for bit in bits:
        order = order + [(keep, flip ^ bit) for keep, flip in order]

    together = [True] * chunks
    blocks = [[], []]
    places = [[], []]
    own = before = None
    for chunk in range(chunks):
        begin = chunk * CHUNK
        own = after(tokens, own)[begin * BLOCK : (begin + CHUNK) * BLOCK]
        pieces = [lax.all_gather(own, "ch", axis=1, tiled=True, axis_index_groups=pairs)]
        for bit in bits:
            pieces = pieces + [swap(piece, "ch", sides, bit) for piece in pieces]
        last = chunk == chunks - 1
        outs = first_section(
            at, pieces, order, begin, CHUNK, w_value, w_gate, first_factor, twiddle, parts, last, together[chunk]
        )
        moved = []
        size = len(outs) // 2 if last else len(outs)
        for part in range(0, len(outs), size):
            if together[chunk]:
                before = exchange([after(outs[part], before)], parts)[0]
                moved.append([before])
            else:
                moved.append(exchange(outs[part : part + size], parts))
        for half in range(2):
            blocks[half].append(moved[half] if last else moved[0])
            places[half].append(0 if last else half)

    def middle(half, begin, indices, splits, way):
        outs = middle_section(
            at, blocks[half], places[half], half, begin, indices,
            second_factor, inverse_first, freq_kernel, row_kernel, parts, splits, way,
        )
        size = len(outs) // splits
        return [exchange(outs[split * size : (split + 1) * size], parts) for split in range(splits)]

    size = max(inner // 2, GROUP)
    starts = list(range(0, inner, size))
    early = [middle(0, start, size, 1, True)[0] for start in starts]
    late = middle(1, 0, inner, 2, True)
    result = last_section(at, early, starts, parts, inverse_second, (tok_rows, channels), 0, 0, None)
    for split, piece in enumerate(late):
        begin = split * (local_rows // len(late))
        result = last_section(at, [piece], [0], parts, inverse_second, (tok_rows, channels), begin, 1, result)
    return result


def solution(mesh):
    return jax.shard_map(
        functools.partial(shards, mesh.shape["tok"], mesh.shape["ch"]),
        mesh=mesh,
        in_specs=(
            P("tok", "ch"),
            P(None, "ch"),
            P(None, "ch"),
            P(),
            P("tok", None),
            P(),
            P("tok", "ch"),
            P(None, "ch"),
            P(),
            P(),
        ),
        out_specs=P("tok", "ch"),
        check_vma=False,
    )
```

```python
import functools

import jax
import jax.numpy as jnp
from jax import lax
from jax.experimental import pallas as pl
from jax.experimental.pallas import tpu as pltpu
from jax.sharding import PartitionSpec as P

BLOCK = 512
CHUNK = 8
GROUP = 16
HALF = 128
STEP = 2
WIDE = 4
VMEM = 56 * 2**20

WHOLE = pl.BlockSpec(memory_space=pltpu.SMEM)


def params():
    return pltpu.CompilerParams(vmem_limit_bytes=VMEM, dimension_semantics=("arbitrary",))


def full(array):
    return pl.BlockSpec(array.shape, lambda s: (0,) * array.ndim)


def wide_dot(left, right):
    return jnp.dot(left, right, preferred_element_type=jnp.float32)


def store_parts(parts_ref, matrix_ref):
    rows = matrix_ref.shape[0]
    matrix = matrix_ref[...]
    upper = matrix.astype(jnp.bfloat16)
    parts_ref[:rows] = upper
    parts_ref[rows:] = (matrix - upper.astype(jnp.float32)).astype(jnp.bfloat16)


def split_dot(parts_ref, right):
    both = wide_dot(parts_ref[...], right)
    rows = both.shape[0] // 2
    return both[:rows] + both[rows:]


def first_body(order, parts, halves, at_ref, *refs):
    count = len(order)
    pieces, (value_ref, gate_ref, factor_ref, twiddle_ref) = refs[:count], refs[count : count + 4]
    outs, (scratch_a, scratch_b, weights, columns) = refs[count + 4 : -4], refs[-4:]
    scratch = (scratch_a, scratch_b)
    step = pl.program_id(0)
    channels = value_ref.shape[1]
    rows = twiddle_ref.shape[0]

    @pl.when(step == 0)
    def _():
        for place, side in enumerate(order):
            begin = pl.multiple_of((at_ref[0] ^ side) * channels, channels)
            here = slice(place * channels, (place + 1) * channels)
            weights[here, :channels] = value_ref[pl.ds(begin, channels), :]
            weights[here, channels:] = gate_ref[pl.ds(begin, channels), :]
        padding = jnp.zeros((128 - rows, BLOCK), jnp.float32)
        columns[...] = jnp.concatenate([twiddle_ref[...], padding], axis=0).T

    both = wide_dot(jnp.concatenate([piece[...] for piece in pieces], axis=1), weights[...])
    value, gate = both[:, :channels], both[:, channels:]
    gated = (value * (gate / (1.0 + jnp.exp(-gate)))).astype(jnp.bfloat16)
    lanes = lax.broadcasted_iota(jnp.int32, columns.shape, 1)
    for row in range(STEP):
        at = step * STEP + row
        scale = jnp.sum(jnp.where(lanes == at, columns[...], 0.0), axis=1, keepdims=True)
        section = wide_dot(factor_ref[...], gated[row * BLOCK : (row + 1) * BLOCK]) * scale
        for half in range(2):
            scratch[half][pl.ds(at, BLOCK, stride=rows), :] = section[:, half * HALF : (half + 1) * HALF]

    @pl.when(step == pl.num_programs(0) - 1)
    def _():
        size = BLOCK // parts * rows
        for part in range(parts):
            for half in range(2):
                block = scratch[half][part * size : (part + 1) * size, :].astype(jnp.bfloat16)
                if halves:
                    outs[half][part] = block
                else:
                    outs[0][part, :, half * HALF : (half + 1) * HALF] = block


def first_section(at, pieces, order, begin, rows, w_value, w_gate, factor, twiddle, parts, halves):
    channels = w_value.shape[1]
    depth, patches = w_value.shape[0], rows * BLOCK
    inner = BLOCK // parts
    widths = [HALF, HALF] if halves else [channels]
    outs = [jax.ShapeDtypeStruct((parts, inner * rows, width), jnp.bfloat16) for width in widths]
    return pl.pallas_call(
        functools.partial(first_body, order, parts, halves),
        grid=(rows // STEP,),
        in_specs=[WHOLE]
        + [
            pl.BlockSpec((STEP * BLOCK, piece.shape[1]), lambda s, start=start: (start // STEP + s, 0))
            for piece, start in zip(pieces, [begin] + [0] * len(pieces))
        ]
        + [full(w_value), full(w_gate), full(factor), pl.BlockSpec((rows, BLOCK), lambda s: (begin // rows, 0))],
        out_specs=[full(out) for out in outs],
        out_shape=outs,
        scratch_shapes=[pltpu.VMEM((BLOCK * rows, HALF), jnp.float32)] * 2
        + [pltpu.VMEM((depth, 2 * channels), jnp.bfloat16), pltpu.VMEM((BLOCK, 128), jnp.float32)],
        compiler_params=params(),
        cost_estimate=pl.CostEstimate(
            flops=2 * patches * channels * (2 * depth + BLOCK),
            bytes_accessed=2 * patches * (depth + channels),
            transcendentals=patches * channels,
        ),
        name="project_and_mix_rows",
    )(at, *pieces, w_value, w_gate, factor, twiddle)


def middle_body(chunks, parts, splits, *refs):
    blocks = refs[:chunks]
    second_ref, inverse_ref, freq_ref, row_ref = refs[chunks : chunks + 4]
    outs, (second, inverse, gathered, scratch) = refs[chunks + 4 : -4], refs[-4:]
    local_rows = chunks * CHUNK

    @pl.when(pl.program_id(0) == 0)
    def _():
        store_parts(second, second_ref)
        store_parts(inverse, inverse_ref)

    @pl.loop(0, GROUP // 2)
    def _(pair):
        start = pl.multiple_of(pair * 2 * CHUNK, 2 * CHUNK)
        lane = pl.multiple_of(pair * 2 * HALF, 2 * HALF)
        for part in range(parts):
            for chunk in range(0, chunks, 2):
                one, two = (
                    blocks[more][part, pl.ds(start, 2 * CHUNK), :].astype(jnp.float32) for more in (chunk, chunk + 1)
                )
                row = part * local_rows + chunk * CHUNK
                for side in range(2):
                    here = slice(side * CHUNK, (side + 1) * CHUNK)
                    tile = jnp.concatenate([one[here], two[here]], axis=0).astype(jnp.bfloat16)
                    gathered[row : row + 2 * CHUNK, pl.ds(pl.multiple_of(lane + side * HALF, HALF), HALF)] = tile

    row_gate = jnp.concatenate([row_ref[...]] * WIDE, axis=1)

    @pl.loop(0, GROUP // WIDE)
    def _(turn):
        lane = pl.multiple_of(turn * WIDE * HALF, WIDE * HALF)
        section = split_dot(second, gathered[:, pl.ds(lane, WIDE * HALF)])
        freq = jnp.concatenate([freq_ref[pl.ds(turn * WIDE + side, 1), :] for side in range(WIDE)], axis=1)
        spectrum = (section * freq * row_gate).astype(jnp.bfloat16)
        section = split_dot(inverse, spectrum)
        for side in range(WIDE):
            scratch[pl.ds(turn * WIDE + side, BLOCK, stride=GROUP), :] = section[:, side * HALF : (side + 1) * HALF]

    inner = BLOCK // parts
    for out, (first, rows) in zip(outs, splits):
        for part in range(parts):
            block = scratch[(part * inner + first) * GROUP : (part * inner + first + rows) * GROUP, :]
            out[part] = block.astype(jnp.bfloat16).reshape(rows, GROUP, HALF)


def middle_section(blocks, places, half, second, inverse, freq, row, parts, splits):
    indices = freq.shape[0]
    outs = [jax.ShapeDtypeStruct((parts, rows, indices, HALF), jnp.bfloat16) for _, rows in splits]
    return pl.pallas_call(
        functools.partial(middle_body, len(blocks), parts, splits),
        grid=(indices // GROUP,),
        in_specs=[
            pl.BlockSpec((parts, GROUP * CHUNK, HALF), lambda s, place=place: (0, s, place)) for place in places
        ]
        + [
            full(second),
            full(inverse),
            pl.BlockSpec((GROUP, HALF), lambda s: (s, half)),
            pl.BlockSpec((BLOCK, HALF), lambda s: (0, half)),
        ],
        out_specs=[pl.BlockSpec((parts, rows, GROUP, HALF), lambda s: (0, 0, s, 0)) for _, rows in splits],
        out_shape=outs,
        scratch_shapes=[pltpu.VMEM((2 * BLOCK, BLOCK), jnp.bfloat16)] * 2
        + [pltpu.VMEM((BLOCK, GROUP * HALF), jnp.bfloat16), pltpu.VMEM((BLOCK * GROUP, HALF), jnp.float32)],
        compiler_params=params(),
        cost_estimate=pl.CostEstimate(
            flops=8 * BLOCK * BLOCK * indices * HALF,
            bytes_accessed=4 * BLOCK * indices * HALF,
            transcendentals=0,
        ),
        name="mix_grid_rows",
    )(*blocks, second, inverse, freq, row)


def last_body(block_ref, inverse_ref, *rest):
    out_ref, inverse, gathered = rest[-3:]
    group = block_ref.shape[1]

    @pl.when(pl.program_id(0) == 0)
    def _():
        store_parts(inverse, inverse_ref)

    for row in range(group):
        gathered[:, row * HALF : (row + 1) * HALF] = block_ref[:, row].reshape(BLOCK, HALF)

    @pl.loop(0, group // WIDE)
    def _(turn):
        lane = pl.multiple_of(turn * WIDE * HALF, WIDE * HALF)
        mixed = split_dot(inverse, gathered[:, pl.ds(lane, WIDE * HALF)]).astype(jnp.bfloat16)
        for side in range(WIDE):
            start = pl.multiple_of((turn * WIDE + side) * BLOCK, BLOCK)
            out_ref[pl.ds(start, BLOCK), :] = mixed[:, side * HALF : (side + 1) * HALF]


def last_section(block, inverse, shape, begin, half, before):
    parts, rows, inner, _ = block.shape
    group = min(rows, 8)
    operands = [block, inverse]
    specs = [pl.BlockSpec((parts, group, inner, HALF), lambda s: (0, s, 0, 0)), full(inverse)]
    aliases = {}
    if before is not None:
        aliases = {len(operands): 0}
        operands.append(before)
        specs.append(pl.BlockSpec(memory_space=pl.ANY))
    return pl.pallas_call(
        last_body,
        grid=(rows // group,),
        in_specs=specs,
        out_specs=pl.BlockSpec((group * BLOCK, HALF), lambda s: (begin // group + s, half)),
        out_shape=jax.ShapeDtypeStruct(shape, jnp.bfloat16),
        input_output_aliases=aliases,
        scratch_shapes=[pltpu.VMEM((2 * BLOCK, BLOCK), jnp.bfloat16), pltpu.VMEM((BLOCK, group * HALF), jnp.bfloat16)],
        compiler_params=params(),
        cost_estimate=pl.CostEstimate(
            flops=4 * BLOCK * BLOCK * rows * HALF,
            bytes_accessed=4 * BLOCK * rows * HALF,
            transcendentals=0,
        ),
        name="mix_rows_back",
    )(*operands)


def swap(x, count, bit):
    return lax.ppermute(x, "ch", [(at, at ^ bit) for at in range(count)])


def exchange(block):
    return lax.all_to_all(block, "tok", split_axis=0, concat_axis=0, tiled=True)


def after(x, before):
    return x if before is None else lax.optimization_barrier((x, before))[0]


def shards(
    parts,
    sides,
    tokens,
    w_value,
    w_gate,
    first_factor,
    twiddle,
    second_factor,
    freq_kernel,
    row_kernel,
    inverse_first,
    inverse_second,
):
    tok_rows, channels = tokens.shape
    local_rows = tok_rows // BLOCK
    chunks = local_rows // CHUNK
    at = lax.axis_index("ch").astype(jnp.int32).reshape(1)
    order = [0]
    bits = [sides >> step for step in range(1, sides.bit_length())]
    for bit in bits:
        order = order + [side ^ bit for side in order]

    size = CHUNK * BLOCK
    owns = [tokens[:size]]
    rest = after(tokens, owns[0])
    owns += [rest[begin : begin + size] for begin in range(size, tok_rows, size)]

    blocks = [[], []]
    places = [[], []]
    before = None
    for chunk, own in enumerate(owns):
        pieces = [own]
        for bit in bits:
            if chunk == 0 and bit == bits[-1]:
                pieces[0] = lax.optimization_barrier((own, *owns[1:]))[0]
            pieces = pieces + [swap(piece, sides, bit) for piece in pieces]
        pieces[0] = tokens
        last = chunk == chunks - 1
        outs = first_section(
            at, pieces, order, chunk * CHUNK, CHUNK, w_value, w_gate, first_factor, twiddle, parts, last
        )
        moved = []
        for out in outs:
            before = exchange(after(out, before))
            moved.append(before)
        for half in range(2):
            blocks[half].append(moved[half if last else 0])
            places[half].append(0 if last else half)

    tail = local_rows // 4
    cuts = [(0, local_rows - tail), (local_rows - tail, tail)] if tail % 8 == 0 else [(0, local_rows)]
    sections = []
    for half, splits in enumerate([[(0, local_rows)], cuts]):
        outs = middle_section(
            blocks[half], places[half], half, second_factor, inverse_first, freq_kernel, row_kernel, parts, splits
        )
        for out, (begin, _) in zip(outs, splits):
            before = exchange(after(out, before))
            sections.append((before, begin, half))
    result = None
    for section, begin, half in sections:
        result = last_section(section, inverse_second, (tok_rows, channels), begin, half, result)
    return result


def solution(mesh):
    return jax.shard_map(
        functools.partial(shards, mesh.shape["tok"], mesh.shape["ch"]),
        mesh=mesh,
        in_specs=(
            P("tok", "ch"),
            P(None, "ch"),
            P(None, "ch"),
            P(),
            P("tok", None),
            P(),
            P("tok", "ch"),
            P(None, "ch"),
            P(),
            P(),
        ),
        out_specs=P("tok", "ch"),
        check_vma=False,
    )
```

```python
import functools

import jax
import jax.numpy as jnp
from jax import lax
from jax.experimental import pallas as pl
from jax.experimental.pallas import tpu as pltpu
from jax.sharding import PartitionSpec as P

BLOCK = 512
CHUNK = 8
GROUP = 16
HALF = 128
STEP = 2
WIDE = 4
VMEM = 56 * 2**20

WHOLE = pl.BlockSpec(memory_space=pltpu.SMEM)


def params():
    return pltpu.CompilerParams(vmem_limit_bytes=VMEM, dimension_semantics=("arbitrary",))


def full(array):
    return pl.BlockSpec(array.shape, lambda s: (0,) * array.ndim)


def wide_dot(left, right):
    return jnp.dot(left, right, preferred_element_type=jnp.float32)


def store_parts(parts_ref, matrix_ref):
    rows = matrix_ref.shape[0]
    matrix = matrix_ref[...]
    upper = matrix.astype(jnp.bfloat16)
    parts_ref[:rows] = upper
    parts_ref[rows:] = (matrix - upper.astype(jnp.float32)).astype(jnp.bfloat16)


def split_dot(parts_ref, right):
    both = wide_dot(parts_ref[...], right)
    rows = both.shape[0] // 2
    return both[:rows] + both[rows:]


def put(outs, half, halves, partner, parts, block):
    lanes = slice(None) if halves else slice(half * HALF, (half + 1) * HALF)
    one_array = len(outs) == (2 if halves else 1)
    if one_array:
        outs[half if halves else 0][partner, :, lanes] = block
    else:
        outs[half * parts + partner if halves else partner][:, lanes] = block


def partner_of(device, partner, parts):
    return device ^ ((parts - partner) % parts)


def place_of(device, partner, parts, together):
    return partner if together else partner_of(device, partner, parts)


def first_body(order, parts, halves, together, at_ref, *refs):
    count = len(order)
    pieces, (value_ref, gate_ref, factor_ref, twiddle_ref) = refs[:count], refs[count : count + 4]
    outs, (scratch_a, scratch_b, weights, columns) = refs[count + 4 : -4], refs[-4:]
    scratch = (scratch_a, scratch_b)
    step = pl.program_id(0)
    channels = value_ref.shape[1]
    rows = twiddle_ref.shape[0]

    @pl.when(step == 0)
    def _():
        for place, side in enumerate(order):
            begin = pl.multiple_of((at_ref[1] ^ side) * channels, channels)
            here = slice(place * channels, (place + 1) * channels)
            weights[here, :channels] = value_ref[pl.ds(begin, channels), :]
            weights[here, channels:] = gate_ref[pl.ds(begin, channels), :]
        padding = jnp.zeros((128 - rows, BLOCK), jnp.float32)
        columns[...] = jnp.concatenate([twiddle_ref[...], padding], axis=0).T

    both = wide_dot(jnp.concatenate([piece[...] for piece in pieces], axis=1), weights[...])
    value, gate = both[:, :channels], both[:, channels:]
    gated = (value * (gate / (1.0 + jnp.exp(-gate)))).astype(jnp.bfloat16)
    lanes = lax.broadcasted_iota(jnp.int32, columns.shape, 1)
    for row in range(STEP):
        at = step * STEP + row
        scale = jnp.sum(jnp.where(lanes == at, columns[...], 0.0), axis=1, keepdims=True)
        section = wide_dot(factor_ref[...], gated[row * BLOCK : (row + 1) * BLOCK]) * scale
        for half in range(2):
            scratch[half][pl.ds(at, BLOCK, stride=rows), :] = section[:, half * HALF : (half + 1) * HALF]

    @pl.when(step == pl.num_programs(0) - 1)
    def _():
        size = BLOCK // parts * rows
        for partner in range(parts):
            begin = pl.multiple_of(place_of(at_ref[0], partner, parts, together) * size, size)
            for half in range(2):
                put(outs, half, halves, partner, parts, scratch[half][pl.ds(begin, size), :].astype(jnp.bfloat16))


def first_section(at, pieces, order, begin, rows, w_value, w_gate, factor, twiddle, parts, halves, together):
    channels = w_value.shape[1]
    depth, patches = w_value.shape[0], rows * BLOCK
    inner = BLOCK // parts
    widths = [HALF] * 2 if halves else [channels]
    if together:
        outs = [jax.ShapeDtypeStruct((parts, inner * rows, width), jnp.bfloat16) for width in widths]
    else:
        outs = [jax.ShapeDtypeStruct((inner * rows, width), jnp.bfloat16) for width in widths for _ in range(parts)]
    return pl.pallas_call(
        functools.partial(first_body, order, parts, halves, together),
        grid=(rows // STEP,),
        in_specs=[WHOLE]
        + [
            pl.BlockSpec((STEP * BLOCK, piece.shape[1]), lambda s, start=start: (start // STEP + s, 0))
            for piece, start in zip(pieces, [begin] + [0] * len(pieces))
        ]
        + [full(w_value), full(w_gate), full(factor), pl.BlockSpec((rows, BLOCK), lambda s: (begin // rows, 0))],
        out_specs=[full(out) for out in outs],
        out_shape=outs,
        scratch_shapes=[pltpu.VMEM((BLOCK * rows, HALF), jnp.float32)] * 2
        + [pltpu.VMEM((depth, 2 * channels), jnp.bfloat16), pltpu.VMEM((BLOCK, 128), jnp.float32)],
        compiler_params=params(),
        cost_estimate=pl.CostEstimate(
            flops=2 * patches * channels * (2 * depth + BLOCK),
            bytes_accessed=2 * patches * (depth + channels),
            transcendentals=patches * channels,
        ),
        name="project_and_mix_rows",
    )(at, *pieces, w_value, w_gate, factor, twiddle)


def middle_body(ways, parts, splits, together, at_ref, *refs):
    chunks = len(ways)
    blocks, count = [], 0
    for way in ways:
        blocks.append(refs[count : count + (1 if way else parts)])
        count += len(blocks[-1])
    second_ref, inverse_ref, freq_ref, row_ref = refs[count : count + 4]
    outs, (second, inverse, gathered, scratch) = refs[count + 4 : -4], refs[-4:]
    local_rows = chunks * CHUNK

    def tile_of(chunk, source, start):
        if ways[chunk]:
            return blocks[chunk][0][source, pl.ds(start, 2 * CHUNK), :].astype(jnp.float32)
        return blocks[chunk][source][pl.ds(start, 2 * CHUNK), :].astype(jnp.float32)

    @pl.when(pl.program_id(0) == 0)
    def _():
        store_parts(second, second_ref)
        store_parts(inverse, inverse_ref)

    @pl.loop(0, GROUP // 2)
    def _(pair):
        start = pl.multiple_of(pair * 2 * CHUNK, 2 * CHUNK)
        lane = pl.multiple_of(pair * 2 * HALF, 2 * HALF)
        for partner in range(parts):
            for chunk in range(0, chunks, 2):
                one, two = (tile_of(chunk + more, partner, start) for more in range(2))
                place = place_of(at_ref[0], partner, parts, ways[chunk])
                row = pl.multiple_of(place * local_rows + chunk * CHUNK, 2 * CHUNK)
                for side in range(2):
                    here = slice(side * CHUNK, (side + 1) * CHUNK)
                    tile = jnp.concatenate([one[here], two[here]], axis=0).astype(jnp.bfloat16)
                    gathered[pl.ds(row, 2 * CHUNK), pl.ds(pl.multiple_of(lane + side * HALF, HALF), HALF)] = tile

    row_gate = jnp.concatenate([row_ref[...]] * WIDE, axis=1)

    @pl.loop(0, GROUP // WIDE)
    def _(turn):
        lane = pl.multiple_of(turn * WIDE * HALF, WIDE * HALF)
        section = split_dot(second, gathered[:, pl.ds(lane, WIDE * HALF)])
        freq = jnp.concatenate([freq_ref[pl.ds(turn * WIDE + side, 1), :] for side in range(WIDE)], axis=1)
        spectrum = (section * freq * row_gate).astype(jnp.bfloat16)
        section = split_dot(inverse, spectrum)
        for side in range(WIDE):
            scratch[pl.ds(turn * WIDE + side, BLOCK, stride=GROUP), :] = section[:, side * HALF : (side + 1) * HALF]

    inner = BLOCK // parts
    for split, (first, rows) in enumerate(splits):
        for partner in range(parts):
            begin = pl.multiple_of((place_of(at_ref[0], partner, parts, together) * inner + first) * GROUP, GROUP)
            block = scratch[pl.ds(begin, rows * GROUP), :].astype(jnp.bfloat16).reshape(rows, GROUP, HALF)
            if together:
                outs[split][partner] = block
            else:
                outs[split * parts + partner][...] = block


def middle_section(at, blocks, places, half, second, inverse, freq, row, parts, splits, together):
    indices = freq.shape[0]
    ways = [len(chunk) == 1 for chunk in blocks]
    operands, specs = [], []
    for chunk, place in zip(blocks, places):
        for block in chunk:
            operands.append(block)
            if len(chunk) == 1:
                specs.append(pl.BlockSpec((parts, GROUP * CHUNK, HALF), lambda s, place=place: (0, s, place)))
            else:
                specs.append(pl.BlockSpec((GROUP * CHUNK, HALF), lambda s, place=place: (s, place)))
    if together:
        outs = [jax.ShapeDtypeStruct((parts, rows, indices, HALF), jnp.bfloat16) for _, rows in splits]
        out_specs = [pl.BlockSpec((parts, rows, GROUP, HALF), lambda s: (0, 0, s, 0)) for _, rows in splits]
    else:
        outs = [jax.ShapeDtypeStruct((rows, indices, HALF), jnp.bfloat16) for _, rows in splits for _ in range(parts)]
        out_specs = [pl.BlockSpec((out.shape[0], GROUP, HALF), lambda s: (0, s, 0)) for out in outs]
    return pl.pallas_call(
        functools.partial(middle_body, ways, parts, splits, together),
        grid=(indices // GROUP,),
        in_specs=[WHOLE]
        + specs
        + [
            full(second),
            full(inverse),
            pl.BlockSpec((GROUP, HALF), lambda s: (s, half)),
            pl.BlockSpec((BLOCK, HALF), lambda s: (0, half)),
        ],
        out_specs=out_specs,
        out_shape=outs,
        scratch_shapes=[pltpu.VMEM((2 * BLOCK, BLOCK), jnp.bfloat16)] * 2
        + [pltpu.VMEM((BLOCK, GROUP * HALF), jnp.bfloat16), pltpu.VMEM((BLOCK * GROUP, HALF), jnp.float32)],
        compiler_params=params(),
        cost_estimate=pl.CostEstimate(
            flops=8 * BLOCK * BLOCK * indices * HALF,
            bytes_accessed=4 * BLOCK * indices * HALF,
            transcendentals=0,
        ),
        name="mix_grid_rows",
    )(at, *operands, second, inverse, freq, row)


def last_body(together, parts, at_ref, *refs):
    count = 1 if together else parts
    blocks, inverse_ref = refs[:count], refs[count]
    out_ref, inverse, gathered = refs[-3:]
    inner = BLOCK // parts
    group = blocks[0].shape[-3]

    @pl.when(pl.program_id(0) == 0)
    def _():
        store_parts(inverse, inverse_ref)

    for row in range(group):
        for partner in range(parts):
            block = blocks[0][partner, row] if together else blocks[partner][row]
            begin = pl.multiple_of(place_of(at_ref[0], partner, parts, together) * inner, inner)
            gathered[pl.ds(begin, inner), row * HALF : (row + 1) * HALF] = block

    @pl.loop(0, group // WIDE)
    def _(turn):
        lane = pl.multiple_of(turn * WIDE * HALF, WIDE * HALF)
        mixed = split_dot(inverse, gathered[:, pl.ds(lane, WIDE * HALF)]).astype(jnp.bfloat16)
        for side in range(WIDE):
            start = pl.multiple_of((turn * WIDE + side) * BLOCK, BLOCK)
            out_ref[pl.ds(start, BLOCK), :] = mixed[:, side * HALF : (side + 1) * HALF]


def last_section(at, blocks, parts, inverse, shape, begin, half, before):
    together = len(blocks) == 1
    rows = blocks[0].shape[-3]
    group = min(rows, 8)
    operands, specs = [at], [WHOLE]
    for block in blocks:
        operands.append(block)
        if together:
            specs.append(pl.BlockSpec((parts, group, *block.shape[2:]), lambda s: (0, s, 0, 0)))
        else:
            specs.append(pl.BlockSpec((group, *block.shape[1:]), lambda s: (s, 0, 0)))
    operands.append(inverse)
    specs.append(full(inverse))
    aliases = {}
    if before is not None:
        aliases = {len(operands): 0}
        operands.append(before)
        specs.append(pl.BlockSpec(memory_space=pl.ANY))
    return pl.pallas_call(
        functools.partial(last_body, together, parts),
        grid=(rows // group,),
        in_specs=specs,
        out_specs=pl.BlockSpec((group * BLOCK, HALF), lambda s: (begin // group + s, half)),
        out_shape=jax.ShapeDtypeStruct(shape, jnp.bfloat16),
        input_output_aliases=aliases,
        scratch_shapes=[pltpu.VMEM((2 * BLOCK, BLOCK), jnp.bfloat16), pltpu.VMEM((BLOCK, group * HALF), jnp.bfloat16)],
        compiler_params=params(),
        cost_estimate=pl.CostEstimate(
            flops=4 * BLOCK * BLOCK * rows * HALF,
            bytes_accessed=4 * BLOCK * rows * HALF,
            transcendentals=0,
        ),
        name="mix_rows_back",
    )(*operands)


def swap(x, count, bit):
    return lax.ppermute(x, "ch", [(at, at ^ bit) for at in range(count)])


def exchange(blocks, parts):
    if len(blocks) == 1:
        return [lax.all_to_all(blocks[0], "tok", split_axis=0, concat_axis=0, tiled=True)]
    moved = list(blocks)
    for partner in range(1, parts):
        bits = partner_of(0, partner, parts)
        moved[partner] = lax.ppermute(blocks[partner], "tok", [(at, at ^ bits) for at in range(parts)])
    return moved


def after(x, before):
    return x if before is None else lax.optimization_barrier((x, before))[0]


def shards(
    parts,
    sides,
    tokens,
    w_value,
    w_gate,
    first_factor,
    twiddle,
    second_factor,
    freq_kernel,
    row_kernel,
    inverse_first,
    inverse_second,
):
    tok_rows, channels = tokens.shape
    local_rows = tok_rows // BLOCK
    chunks = local_rows // CHUNK
    inner = BLOCK // parts
    at = jnp.stack([lax.axis_index("tok"), lax.axis_index("ch")]).astype(jnp.int32)
    order = [0]
    bits = [sides >> step for step in range(1, sides.bit_length())]
    for bit in bits:
        order = order + [side ^ bit for side in order]

    size = CHUNK * BLOCK
    owns = [tokens[:size]]
    rest = after(tokens, owns[0])
    owns += [rest[begin : begin + size] for begin in range(size, tok_rows, size)]

    together = [True] * chunks
    blocks = [[], []]
    places = [[], []]
    before = None
    for chunk, own in enumerate(owns):
        pieces = [own]
        for bit in bits:
            if chunk == 0 and bit == bits[-1]:
                pieces[0] = lax.optimization_barrier((own, *owns[1:]))[0]
            pieces = pieces + [swap(piece, sides, bit) for piece in pieces]
        pieces[0] = tokens
        last = chunk == chunks - 1
        outs = first_section(
            at, pieces, order, chunk * CHUNK, CHUNK, w_value, w_gate, first_factor, twiddle, parts, last, together[chunk]
        )
        moved = []
        size = len(outs) // 2 if last else len(outs)
        for part in range(0, len(outs), size):
            if together[chunk]:
                before = exchange([after(outs[part], before)], parts)[0]
                moved.append([before])
            else:
                moved.append(exchange(outs[part : part + size], parts))
        for half in range(2):
            blocks[half].append(moved[half if last else 0])
            places[half].append(0 if last else half)

    tail = local_rows // 4
    cuts = [(0, local_rows - tail), (local_rows - tail, tail)] if tail % 8 == 0 else [(0, local_rows)]
    sections = []
    for half, splits in enumerate([[(0, local_rows)], cuts]):
        outs = middle_section(
            at, blocks[half], places[half], half,
            second_factor, inverse_first, freq_kernel, row_kernel, parts, splits, False,
        )
        size = len(outs) // len(splits)
        for split, (begin, _) in enumerate(splits):
            outgoing = outs[split * size : (split + 1) * size]
            if split:
                outgoing = [after(out, sections[-1][0][1]) for out in outgoing]
            sections.append((exchange(outgoing, parts), begin, half))
    result = None
    for section, begin, half in sections:
        result = last_section(at, section, parts, inverse_second, (tok_rows, channels), begin, half, result)
    return result


def solution(mesh):
    return jax.shard_map(
        functools.partial(shards, mesh.shape["tok"], mesh.shape["ch"]),
        mesh=mesh,
        in_specs=(
            P("tok", "ch"),
            P(None, "ch"),
            P(None, "ch"),
            P(),
            P("tok", None),
            P(),
            P("tok", "ch"),
            P(None, "ch"),
            P(),
            P(),
        ),
        out_specs=P("tok", "ch"),
        check_vma=False,
    )
```

```python
import functools

import jax
import jax.numpy as jnp
from jax import lax
from jax.experimental import pallas as pl
from jax.experimental.pallas import tpu as pltpu
from jax.sharding import PartitionSpec as P

BLOCK = 512
CHUNK = 8
GROUP = 16
HALF = 128
STEP = 2
WIDE = 4
VMEM = 56 * 2**20

WHOLE = pl.BlockSpec(memory_space=pltpu.SMEM)


def params():
    return pltpu.CompilerParams(vmem_limit_bytes=VMEM, dimension_semantics=("arbitrary",))


def full(array):
    return pl.BlockSpec(array.shape, lambda s: (0,) * array.ndim)


def wide_dot(left, right):
    return jnp.dot(left, right, preferred_element_type=jnp.float32)


def store_parts(parts_ref, matrix_ref):
    rows = matrix_ref.shape[0]
    matrix = matrix_ref[...]
    upper = matrix.astype(jnp.bfloat16)
    parts_ref[:rows] = upper
    parts_ref[rows:] = (matrix - upper.astype(jnp.float32)).astype(jnp.bfloat16)


def split_dot(parts_ref, right):
    both = wide_dot(parts_ref[...], right)
    rows = both.shape[0] // 2
    return both[:rows] + both[rows:]


def first_body(order, parts, halves, at_ref, *refs):
    count = len(order)
    pieces, (value_ref, gate_ref, factor_ref, twiddle_ref) = refs[:count], refs[count : count + 4]
    outs, (scratch_a, scratch_b, weights, columns) = refs[count + 4 : -4], refs[-4:]
    scratch = (scratch_a, scratch_b)
    step = pl.program_id(0)
    channels = value_ref.shape[1]
    rows = twiddle_ref.shape[0]

    @pl.when(step == 0)
    def _():
        for place, side in enumerate(order):
            begin = pl.multiple_of((at_ref[0] ^ side) * channels, channels)
            here = slice(place * channels, (place + 1) * channels)
            weights[here, :channels] = value_ref[pl.ds(begin, channels), :]
            weights[here, channels:] = gate_ref[pl.ds(begin, channels), :]
        padding = jnp.zeros((128 - rows, BLOCK), jnp.float32)
        columns[...] = jnp.concatenate([twiddle_ref[...], padding], axis=0).T

    both = wide_dot(jnp.concatenate([piece[...] for piece in pieces], axis=1), weights[...])
    value, gate = both[:, :channels], both[:, channels:]
    gated = (value * (gate / (1.0 + jnp.exp(-gate)))).astype(jnp.bfloat16)
    lanes = lax.broadcasted_iota(jnp.int32, columns.shape, 1)
    for row in range(STEP):
        at = step * STEP + row
        scale = jnp.sum(jnp.where(lanes == at, columns[...], 0.0), axis=1, keepdims=True)
        section = wide_dot(factor_ref[...], gated[row * BLOCK : (row + 1) * BLOCK]) * scale
        for half in range(2):
            scratch[half][pl.ds(at, BLOCK, stride=rows), :] = section[:, half * HALF : (half + 1) * HALF]

    @pl.when(step == pl.num_programs(0) - 1)
    def _():
        size = BLOCK // parts * rows
        for part in range(parts):
            for half in range(2):
                block = scratch[half][part * size : (part + 1) * size, :].astype(jnp.bfloat16)
                if halves:
                    outs[half][part] = block
                else:
                    outs[0][part, :, half * HALF : (half + 1) * HALF] = block


def first_section(at, pieces, order, begin, rows, w_value, w_gate, factor, twiddle, parts, halves):
    channels = w_value.shape[1]
    depth, patches = w_value.shape[0], rows * BLOCK
    inner = BLOCK // parts
    widths = [HALF, HALF] if halves else [channels]
    outs = [jax.ShapeDtypeStruct((parts, inner * rows, width), jnp.bfloat16) for width in widths]
    return pl.pallas_call(
        functools.partial(first_body, order, parts, halves),
        grid=(rows // STEP,),
        in_specs=[WHOLE]
        + [
            pl.BlockSpec((STEP * BLOCK, piece.shape[1]), lambda s, start=start: (start // STEP + s, 0))
            for piece, start in zip(pieces, [begin] + [0] * len(pieces))
        ]
        + [full(w_value), full(w_gate), full(factor), pl.BlockSpec((rows, BLOCK), lambda s: (begin // rows, 0))],
        out_specs=[full(out) for out in outs],
        out_shape=outs,
        scratch_shapes=[pltpu.VMEM((BLOCK * rows, HALF), jnp.float32)] * 2
        + [pltpu.VMEM((depth, 2 * channels), jnp.bfloat16), pltpu.VMEM((BLOCK, 128), jnp.float32)],
        compiler_params=params(),
        cost_estimate=pl.CostEstimate(
            flops=2 * patches * channels * (2 * depth + BLOCK),
            bytes_accessed=2 * patches * (depth + channels),
            transcendentals=patches * channels,
        ),
        name="project_and_mix_rows",
    )(at, *pieces, w_value, w_gate, factor, twiddle)


def middle_body(chunks, parts, splits, *refs):
    blocks = refs[:chunks]
    second_ref, inverse_ref, freq_ref, row_ref = refs[chunks : chunks + 4]
    outs, (second, inverse, gathered, scratch) = refs[chunks + 4 : -4], refs[-4:]
    local_rows = chunks * CHUNK

    @pl.when(pl.program_id(0) == 0)
    def _():
        store_parts(second, second_ref)
        store_parts(inverse, inverse_ref)

    @pl.loop(0, GROUP // 2)
    def _(pair):
        start = pl.multiple_of(pair * 2 * CHUNK, 2 * CHUNK)
        lane = pl.multiple_of(pair * 2 * HALF, 2 * HALF)
        for part in range(parts):
            for chunk in range(0, chunks, 2):
                one, two = (
                    blocks[more][part, pl.ds(start, 2 * CHUNK), :].astype(jnp.float32) for more in (chunk, chunk + 1)
                )
                row = part * local_rows + chunk * CHUNK
                for side in range(2):
                    here = slice(side * CHUNK, (side + 1) * CHUNK)
                    tile = jnp.concatenate([one[here], two[here]], axis=0).astype(jnp.bfloat16)
                    gathered[row : row + 2 * CHUNK, pl.ds(pl.multiple_of(lane + side * HALF, HALF), HALF)] = tile

    row_gate = jnp.concatenate([row_ref[...]] * WIDE, axis=1)

    @pl.loop(0, GROUP // WIDE, unroll=True)
    def _(turn):
        lane = pl.multiple_of(turn * WIDE * HALF, WIDE * HALF)
        section = split_dot(second, gathered[:, pl.ds(lane, WIDE * HALF)])
        freq = jnp.concatenate([freq_ref[pl.ds(turn * WIDE + side, 1), :] for side in range(WIDE)], axis=1)
        spectrum = (section * freq * row_gate).astype(jnp.bfloat16)
        section = split_dot(inverse, spectrum)
        for side in range(WIDE):
            scratch[pl.ds(turn * WIDE + side, BLOCK, stride=GROUP), :] = section[:, side * HALF : (side + 1) * HALF]

    inner = BLOCK // parts
    for out, (first, rows) in zip(outs, splits):
        for part in range(parts):
            block = scratch[(part * inner + first) * GROUP : (part * inner + first + rows) * GROUP, :]
            out[part] = block.astype(jnp.bfloat16).reshape(rows, GROUP, HALF)


def middle_section(blocks, places, half, second, inverse, freq, row, parts, splits):
    indices = freq.shape[0]
    outs = [jax.ShapeDtypeStruct((parts, rows, indices, HALF), jnp.bfloat16) for _, rows in splits]
    return pl.pallas_call(
        functools.partial(middle_body, len(blocks), parts, splits),
        grid=(indices // GROUP,),
        in_specs=[
            pl.BlockSpec((parts, GROUP * CHUNK, HALF), lambda s, place=place: (0, s, place)) for place in places
        ]
        + [
            full(second),
            full(inverse),
            pl.BlockSpec((GROUP, HALF), lambda s: (s, half)),
            pl.BlockSpec((BLOCK, HALF), lambda s: (0, half)),
        ],
        out_specs=[pl.BlockSpec((parts, rows, GROUP, HALF), lambda s: (0, 0, s, 0)) for _, rows in splits],
        out_shape=outs,
        scratch_shapes=[pltpu.VMEM((2 * BLOCK, BLOCK), jnp.bfloat16)] * 2
        + [pltpu.VMEM((BLOCK, GROUP * HALF), jnp.bfloat16), pltpu.VMEM((BLOCK * GROUP, HALF), jnp.float32)],
        compiler_params=params(),
        cost_estimate=pl.CostEstimate(
            flops=8 * BLOCK * BLOCK * indices * HALF,
            bytes_accessed=4 * BLOCK * indices * HALF,
            transcendentals=0,
        ),
        name="mix_grid_rows",
    )(*blocks, second, inverse, freq, row)


def last_body(block_ref, inverse_ref, *rest):
    out_ref, inverse, gathered = rest[-3:]
    group = block_ref.shape[1]

    @pl.when(pl.program_id(0) == 0)
    def _():
        store_parts(inverse, inverse_ref)

    for row in range(group):
        gathered[:, row * HALF : (row + 1) * HALF] = block_ref[:, row].reshape(BLOCK, HALF)

    @pl.loop(0, group // WIDE, unroll=True)
    def _(turn):
        lane = pl.multiple_of(turn * WIDE * HALF, WIDE * HALF)
        mixed = split_dot(inverse, gathered[:, pl.ds(lane, WIDE * HALF)]).astype(jnp.bfloat16)
        for side in range(WIDE):
            start = pl.multiple_of((turn * WIDE + side) * BLOCK, BLOCK)
            out_ref[pl.ds(start, BLOCK), :] = mixed[:, side * HALF : (side + 1) * HALF]


def last_section(block, inverse, shape, begin, half, before):
    parts, rows, inner, _ = block.shape
    group = min(rows, 8)
    operands = [block, inverse]
    specs = [pl.BlockSpec((parts, group, inner, HALF), lambda s: (0, s, 0, 0)), full(inverse)]
    aliases = {}
    if before is not None:
        aliases = {len(operands): 0}
        operands.append(before)
        specs.append(pl.BlockSpec(memory_space=pl.ANY))
    return pl.pallas_call(
        last_body,
        grid=(rows // group,),
        in_specs=specs,
        out_specs=pl.BlockSpec((group * BLOCK, HALF), lambda s: (begin // group + s, half)),
        out_shape=jax.ShapeDtypeStruct(shape, jnp.bfloat16),
        input_output_aliases=aliases,
        scratch_shapes=[pltpu.VMEM((2 * BLOCK, BLOCK), jnp.bfloat16), pltpu.VMEM((BLOCK, group * HALF), jnp.bfloat16)],
        compiler_params=params(),
        cost_estimate=pl.CostEstimate(
            flops=4 * BLOCK * BLOCK * rows * HALF,
            bytes_accessed=4 * BLOCK * rows * HALF,
            transcendentals=0,
        ),
        name="mix_rows_back",
    )(*operands)


def swap(x, count, bit):
    return lax.ppermute(x, "ch", [(at, at ^ bit) for at in range(count)])


def exchange(block):
    return lax.all_to_all(block, "tok", split_axis=0, concat_axis=0, tiled=True)


def after(x, before):
    return x if before is None else lax.optimization_barrier((x, before))[0]


def shards(
    parts,
    sides,
    tokens,
    w_value,
    w_gate,
    first_factor,
    twiddle,
    second_factor,
    freq_kernel,
    row_kernel,
    inverse_first,
    inverse_second,
):
    tok_rows, channels = tokens.shape
    local_rows = tok_rows // BLOCK
    chunks = local_rows // CHUNK
    at = lax.axis_index("ch").astype(jnp.int32).reshape(1)
    order = [0]
    bits = [sides >> step for step in range(1, sides.bit_length())]
    for bit in bits:
        order = order + [side ^ bit for side in order]

    size = CHUNK * BLOCK
    owns = [tokens[:size]]
    rest = after(tokens, owns[0])
    owns += [rest[begin : begin + size] for begin in range(size, tok_rows, size)]

    blocks = [[], []]
    places = [[], []]
    before = None
    for chunk, own in enumerate(owns):
        pieces = [own]
        for bit in bits:
            if chunk == 0 and bit == bits[-1]:
                pieces[0] = lax.optimization_barrier((own, *owns[1:]))[0]
            pieces = pieces + [swap(piece, sides, bit) for piece in pieces]
        pieces[0] = tokens
        last = chunk == chunks - 1
        outs = first_section(
            at, pieces, order, chunk * CHUNK, CHUNK, w_value, w_gate, first_factor, twiddle, parts, last
        )
        moved = []
        for out in outs:
            before = exchange(after(out, before))
            moved.append(before)
        for half in range(2):
            blocks[half].append(moved[half if last else 0])
            places[half].append(0 if last else half)

    tail = local_rows // 8
    cuts = [(0, local_rows - tail), (local_rows - tail, tail)] if tail % 8 == 0 else [(0, local_rows)]
    sections = []
    for half, splits in enumerate([[(0, local_rows)], cuts]):
        outs = middle_section(
            blocks[half], places[half], half, second_factor, inverse_first, freq_kernel, row_kernel, parts, splits
        )
        sections += [(out, begin, half) for out, (begin, _) in zip(outs, splits)]
    result = None
    moved = []
    for turn, (section, begin, half) in enumerate(sections):
        if turn >= 2:
            out, start, side = moved[turn - 2]
            result = last_section(out, inverse_second, (tok_rows, channels), start, side, result)
            section = after(section, result)
        before = exchange(after(section, before))
        moved.append((before, begin, half))
    for out, start, side in moved[max(len(sections) - 2, 0) :]:
        result = last_section(out, inverse_second, (tok_rows, channels), start, side, result)
    return result


def solution(mesh):
    return jax.shard_map(
        functools.partial(shards, mesh.shape["tok"], mesh.shape["ch"]),
        mesh=mesh,
        in_specs=(
            P("tok", "ch"),
            P(None, "ch"),
            P(None, "ch"),
            P(),
            P("tok", None),
            P(),
            P("tok", "ch"),
            P(None, "ch"),
            P(),
            P(),
        ),
        out_specs=P("tok", "ch"),
        check_vma=False,
    )
```

```python
import functools

import jax
import jax.numpy as jnp
from jax import lax
from jax.experimental import pallas as pl
from jax.experimental.pallas import tpu as pltpu
from jax.sharding import PartitionSpec as P

BLOCK = 512
CHUNK = 8
GROUP = 16
HALF = 128
STEP = 2
WIDE = 4
VMEM = 56 * 2**20

WHOLE = pl.BlockSpec(memory_space=pltpu.SMEM)


def params():
    return pltpu.CompilerParams(vmem_limit_bytes=VMEM, dimension_semantics=("arbitrary",))


def full(array):
    return pl.BlockSpec(array.shape, lambda s: (0,) * array.ndim)


def wide_dot(left, right):
    return jnp.dot(left, right, preferred_element_type=jnp.float32)


def store_parts(parts_ref, matrix_ref):
    rows = matrix_ref.shape[0]
    matrix = matrix_ref[...]
    upper = matrix.astype(jnp.bfloat16)
    parts_ref[:rows] = upper
    parts_ref[rows:] = (matrix - upper.astype(jnp.float32)).astype(jnp.bfloat16)


def split_dot(parts_ref, right):
    both = wide_dot(parts_ref[...], right)
    rows = both.shape[0] // 2
    return both[:rows] + both[rows:]


def first_body(order, parts, halves, at_ref, *refs):
    count = len(order)
    pieces, (value_ref, gate_ref, factor_ref, twiddle_ref) = refs[:count], refs[count : count + 4]
    outs, (scratch_a, scratch_b, weights, columns) = refs[count + 4 : -4], refs[-4:]
    scratch = (scratch_a, scratch_b)
    step = pl.program_id(0)
    channels = value_ref.shape[1]
    rows = twiddle_ref.shape[0]

    @pl.when(step == 0)
    def _():
        for place, side in enumerate(order):
            begin = pl.multiple_of((at_ref[0] ^ side) * channels, channels)
            here = slice(place * channels, (place + 1) * channels)
            weights[here, :channels] = value_ref[pl.ds(begin, channels), :]
            weights[here, channels:] = gate_ref[pl.ds(begin, channels), :]
        padding = jnp.zeros((128 - rows, BLOCK), jnp.float32)
        columns[...] = jnp.concatenate([twiddle_ref[...], padding], axis=0).T

    both = wide_dot(jnp.concatenate([piece[...] for piece in pieces], axis=1), weights[...])
    value, gate = both[:, :channels], both[:, channels:]
    gated = (value * (gate / (1.0 + jnp.exp(-gate)))).astype(jnp.bfloat16)
    lanes = lax.broadcasted_iota(jnp.int32, columns.shape, 1)
    for row in range(STEP):
        at = step * STEP + row
        scale = jnp.sum(jnp.where(lanes == at, columns[...], 0.0), axis=1, keepdims=True)
        section = wide_dot(factor_ref[...], gated[row * BLOCK : (row + 1) * BLOCK]) * scale
        for half in range(2):
            scratch[half][pl.ds(at, BLOCK, stride=rows), :] = section[:, half * HALF : (half + 1) * HALF]

    @pl.when(step == pl.num_programs(0) - 1)
    def _():
        size = BLOCK // parts * rows
        for part in range(parts):
            for half in range(2):
                block = scratch[half][part * size : (part + 1) * size, :].astype(jnp.bfloat16)
                if halves:
                    outs[half][part] = block
                else:
                    outs[0][part, :, half * HALF : (half + 1) * HALF] = block


def first_section(at, pieces, order, begin, rows, w_value, w_gate, factor, twiddle, parts, halves):
    channels = w_value.shape[1]
    depth, patches = w_value.shape[0], rows * BLOCK
    inner = BLOCK // parts
    widths = [HALF, HALF] if halves else [channels]
    outs = [jax.ShapeDtypeStruct((parts, inner * rows, width), jnp.bfloat16) for width in widths]
    return pl.pallas_call(
        functools.partial(first_body, order, parts, halves),
        grid=(rows // STEP,),
        in_specs=[WHOLE]
        + [
            pl.BlockSpec((STEP * BLOCK, piece.shape[1]), lambda s, start=start: (start // STEP + s, 0))
            for piece, start in zip(pieces, [begin] + [0] * len(pieces))
        ]
        + [full(w_value), full(w_gate), full(factor), pl.BlockSpec((rows, BLOCK), lambda s: (begin // rows, 0))],
        out_specs=[full(out) for out in outs],
        out_shape=outs,
        scratch_shapes=[pltpu.VMEM(((BLOCK + 1) * rows, HALF), jnp.float32)] * 2
        + [pltpu.VMEM((depth, 2 * channels), jnp.bfloat16), pltpu.VMEM((BLOCK, 128), jnp.float32)],
        compiler_params=params(),
        cost_estimate=pl.CostEstimate(
            flops=2 * patches * channels * (2 * depth + BLOCK),
            bytes_accessed=2 * patches * (depth + channels),
            transcendentals=patches * channels,
        ),
        name="project_and_mix_rows",
    )(at, *pieces, w_value, w_gate, factor, twiddle)


def middle_body(chunks, parts, splits, *refs):
    blocks = refs[:chunks]
    second_ref, inverse_ref, freq_ref, row_ref = refs[chunks : chunks + 4]
    outs, (second, inverse, gathered, scratch) = refs[chunks + 4 : -4], refs[-4:]
    local_rows = chunks * CHUNK

    @pl.when(pl.program_id(0) == 0)
    def _():
        store_parts(second, second_ref)
        store_parts(inverse, inverse_ref)

    @pl.loop(0, GROUP // 2)
    def _(pair):
        start = pl.multiple_of(pair * 2 * CHUNK, 2 * CHUNK)
        lane = pl.multiple_of(pair * 2 * HALF, 2 * HALF)
        for part in range(parts):
            for chunk in range(0, chunks, 2):
                one, two = (
                    blocks[more][part, pl.ds(start, 2 * CHUNK), :].astype(jnp.float32) for more in (chunk, chunk + 1)
                )
                row = part * local_rows + chunk * CHUNK
                for side in range(2):
                    here = slice(side * CHUNK, (side + 1) * CHUNK)
                    tile = jnp.concatenate([one[here], two[here]], axis=0).astype(jnp.bfloat16)
                    gathered[row : row + 2 * CHUNK, pl.ds(pl.multiple_of(lane + side * HALF, HALF), HALF)] = tile

    row_gate = jnp.concatenate([row_ref[...]] * WIDE, axis=1)

    @pl.loop(0, GROUP // WIDE, unroll=True)
    def _(turn):
        lane = pl.multiple_of(turn * WIDE * HALF, WIDE * HALF)
        section = split_dot(second, gathered[:, pl.ds(lane, WIDE * HALF)])
        freq = jnp.concatenate([freq_ref[pl.ds(turn * WIDE + side, 1), :] for side in range(WIDE)], axis=1)
        spectrum = (section * freq * row_gate).astype(jnp.bfloat16)
        section = split_dot(inverse, spectrum)
        for side in range(WIDE):
            scratch[pl.ds(turn * WIDE + side, BLOCK, stride=GROUP), :] = section[:, side * HALF : (side + 1) * HALF]

    inner = BLOCK // parts
    for out, (first, rows) in zip(outs, splits):
        for part in range(parts):
            block = scratch[(part * inner + first) * GROUP : (part * inner + first + rows) * GROUP, :]
            out[part] = block.astype(jnp.bfloat16).reshape(rows, GROUP, HALF)


def middle_section(blocks, places, half, second, inverse, freq, row, parts, splits):
    indices = freq.shape[0]
    outs = [jax.ShapeDtypeStruct((parts, rows, indices, HALF), jnp.bfloat16) for _, rows in splits]
    return pl.pallas_call(
        functools.partial(middle_body, len(blocks), parts, splits),
        grid=(indices // GROUP,),
        in_specs=[
            pl.BlockSpec((parts, GROUP * CHUNK, HALF), lambda s, place=place: (0, s, place)) for place in places
        ]
        + [
            full(second),
            full(inverse),
            pl.BlockSpec((GROUP, HALF), lambda s: (s, half)),
            pl.BlockSpec((BLOCK, HALF), lambda s: (0, half)),
        ],
        out_specs=[pl.BlockSpec((parts, rows, GROUP, HALF), lambda s: (0, 0, s, 0)) for _, rows in splits],
        out_shape=outs,
        scratch_shapes=[pltpu.VMEM((2 * BLOCK, BLOCK), jnp.bfloat16)] * 2
        + [pltpu.VMEM((BLOCK, GROUP * HALF), jnp.bfloat16), pltpu.VMEM(((BLOCK + 1) * GROUP, HALF), jnp.float32)],
        compiler_params=params(),
        cost_estimate=pl.CostEstimate(
            flops=8 * BLOCK * BLOCK * indices * HALF,
            bytes_accessed=4 * BLOCK * indices * HALF,
            transcendentals=0,
        ),
        name="mix_grid_rows",
    )(*blocks, second, inverse, freq, row)


def last_body(block_ref, inverse_ref, *rest):
    out_ref, inverse, gathered = rest[-3:]
    group = block_ref.shape[1]

    @pl.when(pl.program_id(0) == 0)
    def _():
        store_parts(inverse, inverse_ref)

    for row in range(group):
        gathered[:, row * HALF : (row + 1) * HALF] = block_ref[:, row].reshape(BLOCK, HALF)

    @pl.loop(0, group // WIDE, unroll=True)
    def _(turn):
        lane = pl.multiple_of(turn * WIDE * HALF, WIDE * HALF)
        mixed = split_dot(inverse, gathered[:, pl.ds(lane, WIDE * HALF)]).astype(jnp.bfloat16)
        for side in range(WIDE):
            start = pl.multiple_of((turn * WIDE + side) * BLOCK, BLOCK)
            out_ref[pl.ds(start, BLOCK), :] = mixed[:, side * HALF : (side + 1) * HALF]


def last_section(block, inverse, shape, begin, half, before):
    parts, rows, inner, _ = block.shape
    group = min(rows, 8)
    operands = [block, inverse]
    specs = [pl.BlockSpec((parts, group, inner, HALF), lambda s: (0, s, 0, 0)), full(inverse)]
    aliases = {}
    if before is not None:
        aliases = {len(operands): 0}
        operands.append(before)
        specs.append(pl.BlockSpec(memory_space=pl.ANY))
    return pl.pallas_call(
        last_body,
        grid=(rows // group,),
        in_specs=specs,
        out_specs=pl.BlockSpec((group * BLOCK, HALF), lambda s: (begin // group + s, half)),
        out_shape=jax.ShapeDtypeStruct(shape, jnp.bfloat16),
        input_output_aliases=aliases,
        scratch_shapes=[pltpu.VMEM((2 * BLOCK, BLOCK), jnp.bfloat16), pltpu.VMEM((BLOCK, group * HALF), jnp.bfloat16)],
        compiler_params=params(),
        cost_estimate=pl.CostEstimate(
            flops=4 * BLOCK * BLOCK * rows * HALF,
            bytes_accessed=4 * BLOCK * rows * HALF,
            transcendentals=0,
        ),
        name="mix_rows_back",
    )(*operands)


def swap(x, count, bit):
    return lax.ppermute(x, "ch", [(at, at ^ bit) for at in range(count)])


def exchange(block):
    return lax.all_to_all(block, "tok", split_axis=0, concat_axis=0, tiled=True)


def after(x, before):
    return x if before is None else lax.optimization_barrier((x, before))[0]


def shards(
    parts,
    sides,
    tokens,
    w_value,
    w_gate,
    first_factor,
    twiddle,
    second_factor,
    freq_kernel,
    row_kernel,
    inverse_first,
    inverse_second,
):
    tok_rows, channels = tokens.shape
    local_rows = tok_rows // BLOCK
    chunks = local_rows // CHUNK
    at = lax.axis_index("ch").astype(jnp.int32).reshape(1)
    order = [0]
    bits = [sides >> step for step in range(1, sides.bit_length())]
    for bit in bits:
        order = order + [side ^ bit for side in order]

    size = CHUNK * BLOCK
    owns = [tokens[:size]]
    rest = after(tokens, owns[0])
    owns += [rest[begin : begin + size] for begin in range(size, tok_rows, size)]

    blocks = [[], []]
    places = [[], []]
    before = None
    for chunk, own in enumerate(owns):
        pieces = [own]
        for bit in bits:
            if chunk == 0 and bit == bits[-1]:
                pieces[0] = lax.optimization_barrier((own, *owns[1:]))[0]
            pieces = pieces + [swap(piece, sides, bit) for piece in pieces]
        pieces[0] = tokens
        last = chunk == chunks - 1
        outs = first_section(
            at, pieces, order, chunk * CHUNK, CHUNK, w_value, w_gate, first_factor, twiddle, parts, last
        )
        moved = []
        for out in outs:
            before = exchange(after(out, before))
            moved.append(before)
        for half in range(2):
            blocks[half].append(moved[half if last else 0])
            places[half].append(0 if last else half)

    tail = local_rows // 8
    cuts = [(0, local_rows - tail), (local_rows - tail, tail)] if tail % 8 == 0 else [(0, local_rows)]
    sections = []
    for half, splits in enumerate([[(0, local_rows)], cuts]):
        outs = middle_section(
            blocks[half], places[half], half, second_factor, inverse_first, freq_kernel, row_kernel, parts, splits
        )
        sections += [(out, begin, half) for out, (begin, _) in zip(outs, splits)]
    result = None
    moved = []
    for turn, (section, begin, half) in enumerate(sections):
        if turn >= 2:
            out, start, side = moved[turn - 2]
            result = last_section(out, inverse_second, (tok_rows, channels), start, side, result)
            section = after(section, result)
        before = exchange(after(section, before))
        moved.append((before, begin, half))
    for out, start, side in moved[max(len(sections) - 2, 0) :]:
        result = last_section(out, inverse_second, (tok_rows, channels), start, side, result)
    return result


def solution(mesh):
    return jax.shard_map(
        functools.partial(shards, mesh.shape["tok"], mesh.shape["ch"]),
        mesh=mesh,
        in_specs=(
            P("tok", "ch"),
            P(None, "ch"),
            P(None, "ch"),
            P(),
            P("tok", None),
            P(),
            P("tok", "ch"),
            P(None, "ch"),
            P(),
            P(),
        ),
        out_specs=P("tok", "ch"),
        check_vma=False,
    )
```
